128 devices in a mesh: seq: 32 (over y, x, core), frm: 4 (over z).
Axes of the slice: x: 4, y: 4, z: 4, core: 2. Of those that a mesh axis runs over, the one named last changes fastest.
Arguments:
- hidden_in: bfloat16 [4, 4096, 5120], P('frm', 'seq'), may hold values from -6 to 6
- shift_mod: float32 [5120], replicated, may hold values from -3 to 3
- scale_mod: float32 [5120], replicated, may hold values from -3 to 3
- gate_mod: float32 [5120], replicated, may hold values from 1 to 3
- w_qkv: bfloat16 [5120, 12, 6, 128], P(None, 'frm'), may hold values from -0.078125 to 0.078125
- norm_gain: float32 [12, 4, 128], P('frm'), may hold values from 1.2 to 2.4
- w_out: bfloat16 [12, 2, 128, 5120], P('frm', None, None, 'seq'), may hold values from -0.109375 to 0.109375
- spatial_mask: int32 [12, 4, 32, 32], P('frm'), may hold values from 0 to 1, as said below
- temporal_mask: int32 [12, 32, 4, 4], P('frm'), may hold values from 0 to 1, as said below
- frame_order: int32 [4], replicated, may hold values from 0 to 3, each once
Outputs:
- layer_out: bfloat16 [4, 4096, 5120], P('frm', 'seq')
The draws below stay inside these ranges and needn't reach their ends.
Inputs may be any that keep to these rules, and one draw needn't show every extreme that they name: `spatial_mask`: every block on the diagonal (query block equal to key block) is 1. `temporal_mask`: every entry with the query frame equal to the key frame is 1.
All inputs are finite; a program needn't handle non-finite values.
Results may differ from the reference program's by a relative error of at most 0.018.
Values may be sent and summed in bfloat16 or wider, within the bound.
No kernel may reach another device: no remote copies, remote signals or barrier semaphores. Data moves between devices by JAX's collectives and lax.ppermute only.
A program may use at most 192 MiB of HBM per device.

```python
import math
import jax
import jax.numpy as jnp
from jax import lax

D = 5120
HD = 128
HP = 12
BLK = 128
FRAMES = 4
POSITIONS = 4096
NBLK = 32
N_FRM = 4


def block_mask(key, head_groups, outer, size):
    density_key, pick_key = jax.random.split(key)
    density = jax.random.randint(density_key, (head_groups, 1, 1, 1), 1, 7)
    picks = jax.random.randint(pick_key, (head_groups, outer, size, size), 0, 8)
    diagonal = jnp.arange(size)[:, None] == jnp.arange(size)[None, :]
    return jnp.where((picks < density) | diagonal[None, None], 1, 0).astype(jnp.int32)


def draw_spatial_mask(key, part):
    key = jax.random.fold_in(key, 11)
    return block_mask(key, HP, FRAMES, NBLK)


def draw_temporal_mask(key, part):
    key = jax.random.fold_in(key, 23)
    return block_mask(key, HP, NBLK, FRAMES)


def block_scale(own_key, extent, shards, smallest, high):
    level = 1.0
    for axis_at, parts in shards:
        heights = jax.random.uniform(jax.random.fold_in(jax.random.fold_in(own_key, 6), axis_at), (parts,), jnp.float32, smallest / len(shards), high / len(shards))
        level = level * jnp.repeat(jnp.exp(heights), extent[axis_at] // parts).reshape((-1,) + (1,) * (len(extent) - 1 - axis_at))
    return level


def gaussian(key, extent, scale, bound, cuts=(), kind=jnp.bfloat16):
    drawn = jax.random.normal(key, extent, jnp.float32) * scale
    if len(cuts) > 0:
        drawn = block_scale(key, extent, cuts, -0.22, 0.18) * drawn
    return jnp.clip(drawn, min=-bound, max=bound).astype(kind)


def setup_inputs(seed: int = 0) -> dict:
    streams_of = jax.random.split(jax.random.key(seed), 11)
    hidden_in = gaussian(streams_of[0], (FRAMES, POSITIONS, D), 1.0, 6.0, ((0, 4), (1, 32)))
    shift_mod = gaussian(streams_of[1], (D,), 0.5, 3.0, (), jnp.float32)
    scale_mod = gaussian(streams_of[2], (D,), 0.5, 3.0, (), jnp.float32)
    gate_mod = jnp.clip(jax.random.uniform(streams_of[3], (D,), jnp.float32, 1.0, 3.0), 1.0, 3.0)
    w_qkv = gaussian(streams_of[4], (D, HP, 6, HD), D ** -0.5, 0.078125, ((1, 4),))
    norm_gain = jnp.clip(jnp.exp(math.log(2.4) - 0.6931472 * jax.random.uniform(streams_of[5], (HP, 4, HD), jnp.float32) ** block_scale(streams_of[5], (HP, 4, HD), ((0, 4),), -0.2, 0.2)), 1.2, 2.4)
    w_out = gaussian(streams_of[6], (HP, 2, HD, D), (2 * HP * HD) ** -0.5, 0.109375, ((0, 4), (3, 32)))
    spatial_mask = draw_spatial_mask(jax.random.fold_in(streams_of[10], 71), 0)
    temporal_mask = draw_temporal_mask(jax.random.fold_in(streams_of[10], 71), 0)
    frame_order = jax.random.permutation(streams_of[9], FRAMES).astype(jnp.int32)
    return {"hidden_in": hidden_in, "shift_mod": shift_mod, "scale_mod": scale_mod, "gate_mod": gate_mod, "w_qkv": w_qkv, "norm_gain": norm_gain, "w_out": w_out, "spatial_mask": spatial_mask, "temporal_mask": temporal_mask, "frame_order": frame_order}


def modulate(hidden_in, shift_mod, scale_mod):
    values = hidden_in.astype(jnp.float32)
    centred = values - lax.optimization_barrier(jnp.mean(values, axis=-1, keepdims=True))
    spread = lax.optimization_barrier(jnp.mean(centred * centred, axis=-1, keepdims=True))
    return (centred * lax.rsqrt(spread + 1e-06) * (1.0 + scale_mod) + shift_mod).astype(jnp.bfloat16)

def rms_rows(vectors, gain_row):
    square_mean = lax.optimization_barrier(jnp.mean(vectors * vectors, axis=-1, keepdims=True))
    return (vectors * lax.rsqrt(square_mean + 1e-06) * gain_row).astype(jnp.bfloat16)

def finish_heads(projected, gain_rows):
    return jnp.stack([rms_rows(projected[..., 0, :], gain_rows[..., 0, :]), rms_rows(projected[..., 1, :], gain_rows[..., 1, :]), projected[..., 2, :].astype(jnp.bfloat16), rms_rows(projected[..., 3, :], gain_rows[..., 2, :]), rms_rows(projected[..., 4, :], gain_rows[..., 3, :]), projected[..., 5, :].astype(jnp.bfloat16)], axis=-2)

def rerounded_values(values):
    return lax.optimization_barrier(values.astype(jnp.bfloat16)).astype(jnp.float32)

def regroup_heads(values):
    blocks = POSITIONS // BLK
    return values.reshape(FRAMES, blocks, BLK, HD).transpose(1, 0, 2, 3).reshape(blocks, FRAMES * BLK, HD)

def pair_term(modulated, w_qkv, norm_gain, w_out, spatial_mask, temporal_mask, frame_order, pair_index):
    score_scaling = 1.0 / math.sqrt(HD)
    weights = lax.dynamic_index_in_dim(w_qkv, pair_index, 1, keepdims=False)
    projected = jnp.dot(modulated.reshape(FRAMES * POSITIONS, D), weights.reshape(D, 6 * HD), preferred_element_type=jnp.float32).reshape(FRAMES, POSITIONS, 6, HD)
    gain_rows = lax.dynamic_index_in_dim(norm_gain, pair_index, 0, keepdims=False)
    head_groups = finish_heads(projected, gain_rows).astype(jnp.float32)
    smask = lax.dynamic_index_in_dim(spatial_mask, pair_index, 0, keepdims=False)
    allowed = jnp.repeat(jnp.repeat(smask, BLK, axis=1), BLK, axis=2).astype(jnp.float32)
    scores = jnp.einsum('fqd,fkd->fqk', head_groups[:, :, 0], head_groups[:, :, 1]) * score_scaling
    spatial_weights = jnp.exp(scores) * allowed
    total = lax.optimization_barrier(jnp.sum(spatial_weights, axis=-1))
    summed = jnp.einsum('fqk,fkd->fqd', rerounded_values(spatial_weights), head_groups[:, :, 2])
    spatial_out = (summed / total[..., None]).astype(jnp.bfloat16)
    tmask = lax.dynamic_index_in_dim(temporal_mask, pair_index, 0, keepdims=False)
    allowed_t = jnp.repeat(jnp.repeat(tmask, BLK, axis=1), BLK, axis=2).astype(jnp.float32)
    order = frame_order.astype(jnp.float32)
    distance = jnp.abs(order[:, None] - order[None, :])
    slope = jnp.exp2(-(pair_index.astype(jnp.float32) + 1.0) * 2.0 / HP)
    bias = jnp.repeat(jnp.repeat(slope * distance, BLK, axis=0), BLK, axis=1)
    temporal_scores = jnp.einsum('isl,ivl->isv', regroup_heads(head_groups[:, :, 3]), regroup_heads(head_groups[:, :, 4])) * score_scaling
    temporal_probabilities = jnp.exp(temporal_scores - bias[None]) * allowed_t
    total_t = lax.optimization_barrier(jnp.sum(temporal_probabilities, axis=-1))
    temporal_summed = jnp.einsum('otj,ojp->otp', rerounded_values(temporal_probabilities), regroup_heads(head_groups[:, :, 5]))
    blocks = POSITIONS // BLK
    temporal_out = (temporal_summed / total_t[..., None]).astype(jnp.bfloat16)
    temporal_out = temporal_out.reshape(blocks, FRAMES, BLK, HD).transpose(1, 0, 2, 3).reshape(FRAMES, POSITIONS, HD)
    out_weight = lax.dynamic_index_in_dim(w_out, pair_index, 0, keepdims=False)
    term = jnp.dot(spatial_out.reshape(FRAMES * POSITIONS, HD), out_weight[0], preferred_element_type=jnp.float32)
    term = term + jnp.dot(temporal_out.reshape(FRAMES * POSITIONS, HD), out_weight[1], preferred_element_type=jnp.float32)
    return term

def reference(hidden_in, shift_mod, scale_mod, gate_mod, w_qkv, norm_gain, w_out, spatial_mask, temporal_mask, frame_order):
    modulated = modulate(hidden_in, shift_mod, scale_mod)
    per_group = HP // N_FRM

    def group_step(running, group):
        partial_sum = jnp.zeros((FRAMES * POSITIONS, D), jnp.float32)
        for member in range(per_group):
            pair_index = (group * per_group + member).astype(jnp.int32)
            partial_sum = partial_sum + pair_term(modulated, w_qkv, norm_gain, w_out, spatial_mask, temporal_mask, frame_order, pair_index)
        return (running + rerounded_values(partial_sum), None)
    branch, _ = lax.scan(group_step, jnp.zeros((FRAMES * POSITIONS, D), jnp.float32), jnp.arange(N_FRM, dtype=jnp.int32))
    return (gate_mod * branch.reshape(FRAMES, POSITIONS, D)).astype(jnp.bfloat16)
```

```python
import math

import jax
import jax.numpy as jnp
from jax import lax
from jax.experimental import pallas as pl
from jax.experimental.pallas import tpu as pltpu
from jax.sharding import Mesh, PartitionSpec as P

HP = 12
BLK = 128
HD = 128
EPS = 1e-06
LOG2E = 1.4426950408889634
OFF = -1e30
REL = (0, 1, -1, 2)
VMEM = 56 * 1024 * 1024


def params(limit=VMEM):
    return pltpu.CompilerParams(vmem_limit_bytes=limit)


def whole():
    return pl.BlockSpec(memory_space=pltpu.VMEM)


def cost(flops, size, trans=0):
    return pl.CostEstimate(flops=int(flops), bytes_accessed=int(size), transcendentals=int(trans))


def modulate_kernel(hidden_ref, shift_ref, scale_ref, out_ref):
    values = hidden_ref[...].astype(jnp.float32)
    centred = values - jnp.mean(values, axis=-1, keepdims=True)
    spread = jnp.mean(centred * centred, axis=-1, keepdims=True)
    out_ref[...] = (
        centred * lax.rsqrt(spread + EPS) * (1.0 + scale_ref[...]) + shift_ref[...]
    ).astype(jnp.bfloat16)


def modulate(hidden, shift_mod, scale_mod):
    rows, width = hidden.shape
    step = 32
    return pl.pallas_call(
        modulate_kernel,
        grid=(rows // step,),
        in_specs=[
            pl.BlockSpec((step, width), lambda i: (i, 0)),
            pl.BlockSpec((1, width), lambda i: (0, 0)),
            pl.BlockSpec((1, width), lambda i: (0, 0)),
        ],
        out_specs=pl.BlockSpec((step, width), lambda i: (i, 0)),
        out_shape=jax.ShapeDtypeStruct((rows, width), jnp.bfloat16),
        compiler_params=params(),
        cost_estimate=cost(10 * rows * width, 4 * rows * width),
        name="modulate",
    )(hidden, shift_mod[None], scale_mod[None])


def heads_kernel(parts, aliased, *refs):
    x_refs = refs[:parts]
    w_ref, gain_ref = refs[parts : parts + 2]
    spatial_ref, temporal_ref, rows_ref = refs[parts + 2 + (2 if aliased else 0) :]
    step = pl.program_id(0)
    tokens = x_refs[0].shape[0]

    @pl.when(step == 0)
    def _():
        for part in range(parts):
            rows_ref[pl.ds(part * tokens, tokens), :] = x_refs[part][...]

    projected = jnp.dot(rows_ref[...], w_ref[...], preferred_element_type=jnp.float32)
    which = step % 2
    gains = gain_ref[step // 2]
    gain_pair = jnp.where(which == 0, gains[0:2], gains[2:4])
    vectors = []
    for j in range(2):
        v = projected[:, j * HD : (j + 1) * HD]
        square_mean = jnp.mean(v * v, axis=-1, keepdims=True)
        vectors.append((v * lax.rsqrt(square_mean + EPS) * gain_pair[j : j + 1]).astype(jnp.bfloat16))
    vectors.append(projected[:, 2 * HD :].astype(jnp.bfloat16))

    @pl.when(which == 0)
    def _():
        for j in range(3):
            spatial_ref[:, 0, :, j * HD : (j + 1) * HD] = vectors[j].reshape(parts, tokens, HD)

    @pl.when(which == 1)
    def _():
        for j in range(3):
            temporal_ref[:, 0, :, j * HD : (j + 1) * HD] = vectors[j].reshape(parts, tokens, HD)


def heads(pieces, flat_weight, norm_gain, first, buffers=None):
    parts = len(pieces)
    tokens, width = pieces[0].shape
    pairs = norm_gain.shape[0]
    triple = 3 * HD
    aliased = buffers is not None
    out_spec = pl.BlockSpec((parts, 1, tokens, triple), lambda n: (first // parts, n // 2, 0, 0))
    in_specs = [pl.BlockSpec((tokens, width), lambda n: (0, 0)) for _ in pieces]
    in_specs += [
        pl.BlockSpec((width, triple), lambda n: (0, n)),
        pl.BlockSpec(norm_gain.shape, lambda n: (0, 0, 0)),
    ]
    args = list(pieces) + [flat_weight, norm_gain]
    aliases = {}
    if aliased:
        in_specs += [pl.BlockSpec(memory_space=pl.ANY)] * 2
        aliases = {len(args): 0, len(args) + 1: 1}
        args += list(buffers)

    def body(*refs):
        heads_kernel(parts, aliased, *refs)

    return pl.pallas_call(
        body,
        grid=(2 * pairs,),
        in_specs=in_specs,
        out_specs=[out_spec, out_spec],
        out_shape=[
            jax.ShapeDtypeStruct((4, 4, tokens, triple), jnp.bfloat16),
            jax.ShapeDtypeStruct((4, pairs, tokens, triple), jnp.bfloat16),
        ],
        scratch_shapes=[pltpu.VMEM((parts * tokens, width), jnp.bfloat16)],
        input_output_aliases=aliases,
        compiler_params=params(),
        cost_estimate=cost(
            2 * parts * tokens * width * 2 * pairs * triple, width * 2 * pairs * triple * 2
        ),
        name="qkv_heads",
    )(*args)


def spatial_kernel(chunk, own_ref, other_ref, bias_ref, out_ref, keys_ref, values_ref):
    blocks = own_ref.shape[0]
    half = blocks * BLK
    step = pl.program_id(0)

    @pl.when(step == 0)
    def _():
        for at, ref in ((0, own_ref), (half, other_ref)):
            keys_ref[pl.ds(at, half), :] = ref[:, :, HD : 2 * HD].reshape(half, HD)
            values_ref[pl.ds(at, half), 0:HD] = ref[:, :, 2 * HD :].reshape(half, HD)
        values_ref[:, HD:] = jnp.ones((2 * half, HD), jnp.bfloat16)

    per_step = out_ref.shape[0]
    rows = per_step * BLK
    queries = own_ref[pl.ds(step * per_step, per_step), :, 0:HD].reshape(rows, HD)
    factor = LOG2E / math.sqrt(HD)
    summed = jnp.zeros((rows, 2 * HD), jnp.float32)
    for at in range(0, 2 * half, chunk):
        scores = lax.dot_general(
            queries, keys_ref[at : at + chunk, :], (((1,), (1,)), ((), ())),
            preferred_element_type=jnp.float32,
        )
        bias = bias_ref[:, :, at : at + chunk]
        scores = scores.reshape(per_step, BLK, chunk) * factor + bias
        weights = jnp.exp2(scores).astype(jnp.bfloat16).reshape(rows, chunk)
        summed = summed + jnp.dot(
            weights, values_ref[at : at + chunk, :], preferred_element_type=jnp.float32
        )
    out_ref[...] = (
        (summed[:, :HD] / summed[:, HD:]).astype(jnp.bfloat16).reshape(per_step, BLK, HD)
    )


def spatial_attention(own, other, bias):
    blocks, tokens, triple = own.shape
    per_step = 4
    total = 2 * blocks * tokens
    return pl.pallas_call(
        lambda *refs: spatial_kernel(512, *refs),
        grid=(blocks // per_step,),
        in_specs=[
            pl.BlockSpec((blocks, tokens, triple), lambda i: (0, 0, 0)),
            pl.BlockSpec((blocks, tokens, triple), lambda i: (0, 0, 0)),
            pl.BlockSpec((per_step, 1, total), lambda i: (i, 0, 0)),
        ],
        out_specs=pl.BlockSpec((per_step, tokens, HD), lambda i: (i, 0, 0)),
        out_shape=jax.ShapeDtypeStruct((blocks, tokens, HD), jnp.bfloat16),
        scratch_shapes=[
            pltpu.VMEM((total, HD), jnp.bfloat16),
            pltpu.VMEM((total, 2 * HD), jnp.bfloat16),
        ],
        compiler_params=params(),
        cost_estimate=cost(
            6 * blocks * tokens * total * HD, 4 * blocks * tokens * triple, blocks * tokens * total
        ),
        name="spatial_attention",
    )(own, other, bias)


def temporal_kernel(qkv_ref, bias_ref, out_ref):
    frames, _, tokens, _ = qkv_ref.shape
    rows = frames * tokens
    factor = LOG2E / math.sqrt(HD)
    queries = qkv_ref[:, 0, :, 0:HD].reshape(rows, HD)
    keys = qkv_ref[:, 0, :, HD : 2 * HD].reshape(rows, HD)
    values = qkv_ref[:, 0, :, 2 * HD :].reshape(rows, HD)
    values = jnp.concatenate([values, jnp.ones((rows, HD), jnp.bfloat16)], axis=1)
    scores = lax.dot_general(
        queries, keys, (((1,), (1,)), ((), ())), preferred_element_type=jnp.float32
    )
    scores = scores.reshape(frames, tokens, rows) * factor + bias_ref[0]
    weights = jnp.exp2(scores).astype(jnp.bfloat16).reshape(rows, rows)
    summed = jnp.dot(weights, values, preferred_element_type=jnp.float32)
    result = (summed[:, :HD] / summed[:, HD:]).astype(jnp.bfloat16)
    out_ref[:, 0] = result.reshape(frames, tokens, HD)


def temporal_attention(qkv, bias):
    frames, pairs, tokens, triple = qkv.shape
    rows = frames * tokens
    return pl.pallas_call(
        temporal_kernel,
        grid=(pairs,),
        in_specs=[
            pl.BlockSpec((frames, 1, tokens, triple), lambda h: (0, h, 0, 0)),
            pl.BlockSpec((1, frames, 1, rows), lambda h: (h, 0, 0, 0)),
        ],
        out_specs=pl.BlockSpec((frames, 1, tokens, HD), lambda h: (0, h, 0, 0)),
        out_shape=jax.ShapeDtypeStruct((frames, pairs, tokens, HD), jnp.bfloat16),
        compiler_params=params(),
        cost_estimate=cost(6 * pairs * rows * rows * HD, 2 * frames * pairs * tokens * triple),
        name="temporal_attention",
    )(qkv, bias)


def project_kernel(groups_ref, own_ref, other_ref, w_ref, gate_ref, mine_ref, theirs_ref, rows_ref):
    slots, kinds, pairs, tokens, _ = own_ref.shape
    step = pl.program_id(0)

    @pl.when(step == 0)
    def _():
        for at, ref in ((0, own_ref), (tokens, other_ref)):
            for slot in range(slots):
                for pair in range(pairs):
                    for kind in range(kinds):
                        col = (pair * kinds + kind) * HD
                        rows_ref[slot, at : at + tokens, col : col + HD] = ref[slot, kind, pair]

    branch = jnp.zeros((2 * tokens, w_ref.shape[1]), jnp.float32)
    for slot in range(slots):
        partial = lax.dot_general(
            rows_ref[slot], w_ref[groups_ref[slot]], (((1,), (1,)), ((), ())),
            preferred_element_type=jnp.float32,
        )
        branch = branch + partial.astype(jnp.bfloat16).astype(jnp.float32)
    result = (branch * gate_ref[...]).astype(jnp.bfloat16)
    mine_ref[...] = result[:tokens]
    theirs_ref[...] = result[tokens:]


def project(group_ids, own, other, weight, gate):
    slots, kinds, pairs, tokens, _ = own.shape
    groups, columns, depth = weight.shape
    step = 640
    whole_block = pl.BlockSpec(own.shape, lambda n, ids: (0, 0, 0, 0, 0))
    out_spec = pl.BlockSpec((tokens, step), lambda n, ids: (0, n))
    return pl.pallas_call(
        project_kernel,
        grid_spec=pltpu.PrefetchScalarGridSpec(
            num_scalar_prefetch=1,
            grid=(columns // step,),
            in_specs=[
                whole_block,
                whole_block,
                pl.BlockSpec((groups, step, depth), lambda n, ids: (0, n, 0)),
                pl.BlockSpec((1, step), lambda n, ids: (0, n)),
            ],
            out_specs=[out_spec, out_spec],
            scratch_shapes=[pltpu.VMEM((slots, 2 * tokens, depth), jnp.bfloat16)],
        ),
        out_shape=[jax.ShapeDtypeStruct((tokens, columns), jnp.bfloat16)] * 2,
        compiler_params=params(),
        cost_estimate=cost(
            4 * tokens * columns * depth * groups, 2 * groups * columns * depth
        ),
        name="project",
    )(group_ids, own, other, weight, gate)


def local(
    hidden_in,
    shift_mod,
    scale_mod,
    gate_mod,
    w_qkv,
    norm_gain,
    w_out,
    spatial_mask,
    temporal_mask,
    frame_order,
):
    width = hidden_in.shape[2]
    tokens = hidden_in.shape[1]
    pairs = w_qkv.shape[1]
    y, x, core, z = (lax.axis_index(name) for name in ("y", "x", "core", "frm"))
    chips = lax.axis_size("y") * lax.axis_size("x")
    planes = lax.axis_size("frm")
    chip = y * lax.axis_size("x") + x
    seq_index = chip * 2 + core

    def along_z(value, shift):
        return lax.ppermute(value, "frm", [(i, (i + shift) % planes) for i in range(planes)])

    def swap_cores(value):
        return lax.ppermute(value, "core", [(0, 1), (1, 0)])

    with jax.named_scope("gather_w_out"):
        columns = w_out.shape[3]
        turned = jnp.transpose(w_out.reshape(pairs * 2 * HD, columns))
        turned = lax.ppermute(
            turned,
            ("y", "x", "core"),
            [(s, (s % chips) * 2 + s // chips) for s in range(2 * chips)],
        )
        full_out = lax.all_gather(turned, ("frm", "y", "x"), axis=0, tiled=False)
        full_out = full_out.reshape(planes, chips * columns, pairs * 2 * HD)

    with jax.named_scope("modulate"):
        own = modulate(hidden_in[0], shift_mod, scale_mod)

    with jax.named_scope("hidden_over_z"):
        after = along_z(own, -1)
        before = along_z(own, 1)
        cut = tokens // 2
        far_low = along_z(before[:cut], 1)
        far_high = along_z(after[cut:], -1)
        far = jnp.concatenate([far_low, far_high], axis=0)

    with jax.named_scope("qkv"):
        flat_weight = w_qkv.reshape(width, pairs * 6 * HD)
        buffers = heads([own, after, before], flat_weight, norm_gain, 0)
        spatial, temporal = heads([far], flat_weight, norm_gain, 3, buffers)

    frames = (z + jnp.array(REL, jnp.int32)) % planes

    with jax.named_scope("temporal"):
        order = frame_order.astype(jnp.float32)[frames]
        distance = jnp.abs(order[:, None] - order[None, :])
        pair_global = (z * pairs + jnp.arange(pairs, dtype=jnp.int32)).astype(jnp.float32)
        slope = jnp.exp2(-(pair_global + 1.0) * 2.0 / HP)
        tmask = lax.dynamic_index_in_dim(temporal_mask, seq_index, 1, keepdims=False)
        tmask = tmask[:, frames][:, :, frames]
        bias_t = jnp.where(tmask > 0, -slope[:, None, None] * distance[None] * LOG2E, OFF)
        bias_t = jnp.repeat(bias_t, tokens, axis=2)[:, :, None, :]
        temporal_out = temporal_attention(temporal, bias_t)

    with jax.named_scope("spatial"):
        smask = lax.dynamic_index_in_dim(
            spatial_mask, jnp.minimum(x, pairs - 1), 0, keepdims=False
        )
        slot_frame = (z + jnp.array(REL, jnp.int32)[y]) % planes
        smask = lax.dynamic_index_in_dim(smask, slot_frame, 0, keepdims=False)
        smask = smask.reshape(chips, 2, chips, 2)
        smask = lax.dynamic_index_in_dim(smask, core, 1, keepdims=False)
        own_keys = lax.dynamic_index_in_dim(smask, core, 2, keepdims=False)
        other_keys = lax.dynamic_index_in_dim(smask, 1 - core, 2, keepdims=False)
        smask = jnp.concatenate([own_keys, other_keys], axis=1)
        bias_s = jnp.repeat(jnp.where(smask > 0, 0.0, OFF).astype(jnp.float32), BLK, axis=1)
        mine = lax.all_to_all(
            spatial.reshape(chips, tokens, 3 * HD), ("y", "x"), 0, 0, tiled=True
        )
        other = swap_cores(mine)
        spatial_out = spatial_attention(mine, other, bias_s[:, None, :])
        spatial_out = lax.all_to_all(spatial_out, ("y", "x"), 0, 0, tiled=True)
        spatial_out = spatial_out.reshape(4, 4, tokens, HD)[:, :pairs]

    with jax.named_scope("heads_to_frames"):
        both = jnp.stack([spatial_out, temporal_out], axis=1)
        moved = [both[0]] + [along_z(both[i], REL[i]) for i in range(1, 4)]
        moved = jnp.stack(moved)
        other_heads = swap_cores(moved)

    with jax.named_scope("project"):
        group_ids = (z - jnp.array(REL, jnp.int32)) % planes
        half = chips * columns
        gate = lax.dynamic_slice_in_dim(gate_mod, core * half, half)[None]
        out_mine, out_theirs = project(group_ids, moved, other_heads, full_out, gate)
        received = swap_cores(out_theirs)
        left = jnp.where(core == 0, out_mine, received)
        right = jnp.where(core == 0, received, out_mine)
        return jnp.concatenate([left, right], axis=1)[None]


def solution(mesh):
    split = Mesh(mesh.devices.reshape(4, 4, 2, 4), ("y", "x", "core", "frm"))
    seq = ("y", "x", "core")
    placed = (
        P("frm", seq, None),
        P(),
        P(),
        P(),
        P(None, "frm", None, None),
        P("frm", None, None),
        P("frm", None, None, seq),
        P("frm", None, None, None),
        P("frm", None, None, None),
        P(),
    )
    return jax.shard_map(
        local, mesh=split, in_specs=placed, out_specs=P("frm", seq, None), check_vma=False
    )
```

```python
import math

import jax
import jax.numpy as jnp
from jax import lax
from jax.experimental import pallas as pl
from jax.experimental.pallas import tpu as pltpu
from jax.sharding import Mesh, PartitionSpec as P

HP = 12
BLK = 128
HD = 128
EPS = 1e-06
LOG2E = 1.4426950408889634
OFF = -1e30
REL = (0, 2, 1, -1)
VMEM = 56 * 1024 * 1024


def params(limit=VMEM):
    return pltpu.CompilerParams(vmem_limit_bytes=limit)


def whole():
    return pl.BlockSpec(memory_space=pltpu.VMEM)


def cost(flops, size, trans=0):
    return pl.CostEstimate(flops=int(flops), bytes_accessed=int(size), transcendentals=int(trans))


def modulate_kernel(hidden_ref, shift_ref, scale_ref, out_ref):
    values = hidden_ref[...].astype(jnp.float32)
    centred = values - jnp.mean(values, axis=-1, keepdims=True)
    spread = jnp.mean(centred * centred, axis=-1, keepdims=True)
    out_ref[...] = (
        centred * lax.rsqrt(spread + EPS) * (1.0 + scale_ref[...]) + shift_ref[...]
    ).astype(jnp.bfloat16)


def modulate(hidden, shift_mod, scale_mod, step=64):
    rows, width = hidden.shape
    return pl.pallas_call(
        modulate_kernel,
        grid=(rows // step,),
        in_specs=[
            pl.BlockSpec((step, width), lambda i: (i, 0)),
            pl.BlockSpec((1, width), lambda i: (0, 0)),
            pl.BlockSpec((1, width), lambda i: (0, 0)),
        ],
        out_specs=pl.BlockSpec((step, width), lambda i: (i, 0)),
        out_shape=jax.ShapeDtypeStruct((rows, width), jnp.bfloat16),
        compiler_params=params(),
        cost_estimate=cost(10 * rows * width, 4 * rows * width),
        name="modulate",
    )(hidden, shift_mod[None], scale_mod[None])


def heads_kernel(parts, aliased, *refs):
    x_refs = refs[:parts]
    w_ref, gain_ref = refs[parts : parts + 2]
    out_ref, rows_ref = refs[parts + 2 + aliased :]
    pair = pl.program_id(0)
    frames, _, tokens, _ = out_ref.shape

    @pl.when(pair == 0)
    def _():
        at = 0
        for ref in x_refs:
            rows_ref[at : at + ref.shape[0], :] = ref[...]
            at += ref.shape[0]

    weight = jnp.concatenate([w_ref[0, j] for j in range(3)], axis=1)
    projected = jnp.dot(rows_ref[...], weight, preferred_element_type=jnp.float32)
    gains = gain_ref[pair]
    for j in range(3):
        v = projected[:, j * HD : (j + 1) * HD]
        if j < 2:
            square_mean = jnp.mean(v * v, axis=-1, keepdims=True)
            v = v * lax.rsqrt(square_mean + EPS) * gains[j : j + 1]
        out_ref[:, 0, :, j * HD : (j + 1) * HD] = v.astype(jnp.bfloat16).reshape(
            frames, tokens, HD
        )


def heads(pieces, weight, norm_gain, kind, slots, first, buffer=None):
    parts = len(pieces)
    width = pieces[0].shape[1]
    rows = sum(piece.shape[0] for piece in pieces)
    pairs = weight.shape[0]
    frames = rows // BLK
    triple = 3 * HD
    aliased = buffer is not None
    in_specs = [pl.BlockSpec(piece.shape, lambda n: (0, 0)) for piece in pieces]
    in_specs += [
        pl.BlockSpec((1, 3, width, HD), lambda n: (n, kind, 0, 0)),
        pl.BlockSpec((pairs, 2, HD), lambda n: (0, 0, 0)),
    ]
    args = list(pieces) + [weight, norm_gain[kind]]
    aliases = {}
    if aliased:
        in_specs.append(pl.BlockSpec(memory_space=pl.ANY))
        aliases = {len(args): 0}
        args.append(buffer)

    def body(*refs):
        heads_kernel(parts, int(aliased), *refs)

    return pl.pallas_call(
        body,
        grid=(pairs,),
        in_specs=in_specs,
        out_specs=pl.BlockSpec((frames, 1, BLK, triple), lambda n: (first // frames, n, 0, 0)),
        out_shape=jax.ShapeDtypeStruct((4, slots, BLK, triple), jnp.bfloat16),
        scratch_shapes=[pltpu.VMEM((rows, width), jnp.bfloat16)],
        input_output_aliases=aliases,
        compiler_params=params(),
        cost_estimate=cost(2 * rows * width * pairs * triple, width * pairs * triple * 2),
        name="qkv_spatial" if kind == 0 else "qkv_temporal",
    )(*args)


def spatial_kernel(chunk, own_ref, other_ref, bias_ref, out_ref, keys_ref, values_ref):
    blocks = own_ref.shape[0]
    half = blocks * BLK
    step = pl.program_id(0)

    @pl.when(step == 0)
    def _():
        for at, ref in ((0, own_ref), (half, other_ref)):
            keys_ref[pl.ds(at, half), 0:HD] = ref[:, :, HD : 2 * HD].reshape(half, HD)
            values_ref[pl.ds(at, half), 0:HD] = ref[:, :, 2 * HD :].reshape(half, HD)
        values_ref[:, HD:] = jnp.ones((2 * half, HD), jnp.bfloat16)
        for block in range(2 * blocks):
            row = jnp.broadcast_to(bias_ref[block : block + 1, :], (BLK, HD))
            keys_ref[block * BLK : (block + 1) * BLK, HD:] = row.astype(jnp.bfloat16)

    per_step = out_ref.shape[0]
    rows = per_step * BLK
    lane = lax.broadcasted_iota(jnp.int32, (per_step, BLK, HD), 2)
    block_at = lax.broadcasted_iota(jnp.int32, (per_step, BLK, HD), 0) + step * per_step
    one_hot = jnp.where(lane == block_at, 1.0, 0.0).astype(jnp.bfloat16)
    queries = own_ref[pl.ds(step * per_step, per_step), :, 0:HD]
    queries = jnp.concatenate([queries, one_hot], axis=2).reshape(rows, 2 * HD)
    summed = jnp.zeros((rows, 2 * HD), jnp.float32)
    for at in range(0, 2 * half, chunk):
        scores = lax.dot_general(
            queries, keys_ref[at : at + chunk, :], (((1,), (1,)), ((), ())),
            preferred_element_type=jnp.float32,
        )
        weights = jnp.exp2(scores).astype(jnp.bfloat16)
        summed = summed + jnp.dot(
            weights, values_ref[at : at + chunk, :], preferred_element_type=jnp.float32
        )
    out_ref[...] = (
        (summed[:, :HD] / summed[:, HD:]).astype(jnp.bfloat16).reshape(per_step, BLK, HD)
    )


def spatial_attention(own, other, bias, per_step=16, chunk=512):
    blocks, tokens, triple = own.shape
    total = 2 * blocks * tokens
    return pl.pallas_call(
        lambda *refs: spatial_kernel(chunk, *refs),
        grid=(blocks // per_step,),
        in_specs=[
            pl.BlockSpec((blocks, tokens, triple), lambda i: (0, 0, 0)),
            pl.BlockSpec((blocks, tokens, triple), lambda i: (0, 0, 0)),
            pl.BlockSpec((2 * blocks, HD), lambda i: (0, 0)),
        ],
        out_specs=pl.BlockSpec((per_step, tokens, HD), lambda i: (i, 0, 0)),
        out_shape=jax.ShapeDtypeStruct((blocks, tokens, HD), jnp.bfloat16),
        scratch_shapes=[
            pltpu.VMEM((total, 2 * HD), jnp.bfloat16),
            pltpu.VMEM((total, 2 * HD), jnp.bfloat16),
        ],
        compiler_params=params(),
        cost_estimate=cost(
            8 * blocks * tokens * total * HD, 4 * blocks * tokens * triple, blocks * tokens * total
        ),
        name="spatial_attention",
    )(own, other, bias)


def temporal_kernel(qkv_ref, bias_ref, out_ref):
    frames, _, tokens, _ = qkv_ref.shape
    rows = frames * tokens
    queries = qkv_ref[:, 0, :, 0:HD].reshape(rows, HD)
    keys = qkv_ref[:, 0, :, HD : 2 * HD].reshape(rows, HD)
    values = qkv_ref[:, 0, :, 2 * HD :].reshape(rows, HD)
    values = jnp.concatenate([values, jnp.ones((rows, HD), jnp.bfloat16)], axis=1)
    scores = lax.dot_general(
        queries, keys, (((1,), (1,)), ((), ())), preferred_element_type=jnp.float32
    )
    scores = scores.reshape(frames, tokens, rows) + bias_ref[0]
    weights = jnp.exp2(scores).astype(jnp.bfloat16).reshape(rows, rows)
    summed = jnp.dot(weights, values, preferred_element_type=jnp.float32)
    result = (summed[:, :HD] / summed[:, HD:]).astype(jnp.bfloat16)
    out_ref[:, 0] = result.reshape(frames, tokens, HD)


def temporal_attention(qkv, bias):
    frames, pairs, tokens, triple = qkv.shape
    rows = frames * tokens
    return pl.pallas_call(
        temporal_kernel,
        grid=(pairs,),
        in_specs=[
            pl.BlockSpec((frames, 1, tokens, triple), lambda h: (0, h, 0, 0)),
            pl.BlockSpec((1, frames, 1, rows), lambda h: (h, 0, 0, 0)),
        ],
        out_specs=pl.BlockSpec((frames, 1, tokens, HD), lambda h: (0, h, 0, 0)),
        out_shape=jax.ShapeDtypeStruct((frames, pairs, tokens, HD), jnp.bfloat16),
        compiler_params=params(),
        cost_estimate=cost(6 * pairs * rows * rows * HD, 2 * frames * pairs * tokens * triple),
        name="temporal_attention",
    )(qkv, bias)


OWN_SLOT = {0: 0, 1: 2, -1: 3}
FAR_SLOT = {0: 0, 1: 2, -1: 1}


def project_kernel(which, *refs):
    spatial_ref, temporal_ref, w_ref = refs[:3]
    partial_refs, (kept_ref, sent_ref, rows_ref) = refs[3:-3], refs[-3:]
    step = pl.program_id(0)
    shards, _, pairs, kinds, columns, _ = w_ref.shape
    slot_of = (OWN_SLOT, FAR_SLOT)[which]

    @pl.when(step == 0)
    def _():
        for number, target in enumerate((0, 1, -1)):
            for kind, ref in enumerate((spatial_ref, temporal_ref)):
                for pair in range(pairs):
                    at = (pair * kinds + kind) * HD
                    rows_ref[number, :, at : at + HD] = ref[slot_of[target], pair]

    weight = jnp.concatenate(
        [
            w_ref[:, 0, pair, kind].reshape(shards * columns, HD)
            for pair in range(pairs)
            for kind in range(kinds)
        ],
        axis=1,
    )
    neighbour = 1 + step * 2 // pl.num_programs(0)
    rows = jnp.concatenate([rows_ref[0], rows_ref[neighbour]], axis=0)
    product = lax.dot_general(
        rows, weight, (((1,), (1,)), ((), ())), preferred_element_type=jnp.float32
    )
    kept, sent = product[:BLK], product[BLK:]
    if partial_refs:
        kept = kept + partial_refs[0][...]
        sent = sent + partial_refs[1][...]
    kept_ref[...] = kept
    sent_ref[...] = sent.astype(sent_ref.dtype)


def project(which, spatial, temporal, weight, partials=()):
    shards, _, pairs, kinds, shard, _ = weight.shape
    per_step = 8
    steps, width = shards // per_step, per_step * shard
    depth = kinds * pairs * HD
    column = pl.BlockSpec((BLK, width), lambda n: (0, n))
    return pl.pallas_call(
        lambda *refs: project_kernel(which, *refs),
        grid=(steps,),
        in_specs=[
            pl.BlockSpec(spatial.shape, lambda n: (0, 0, 0, 0)),
            pl.BlockSpec(temporal.shape, lambda n: (0, 0, 0, 0)),
            pl.BlockSpec(
                (per_step, 1, pairs, kinds, shard, HD), lambda n: (n, which, 0, 0, 0, 0)
            ),
        ]
        + [column] * len(partials),
        out_specs=[column, column],
        out_shape=[
            jax.ShapeDtypeStruct((BLK, steps * width), jnp.float32),
            jax.ShapeDtypeStruct(
                (BLK, steps * width), jnp.bfloat16 if partials else jnp.float32
            ),
        ],
        scratch_shapes=[pltpu.VMEM((3, BLK, depth), jnp.bfloat16)],
        compiler_params=params(),
        cost_estimate=cost(4 * BLK * steps * width * depth, 2 * steps * width * depth),
        name=("project_own_group", "project_far_group")[which],
    )(spatial, temporal, weight, *partials)


def combine_kernel(own_ref, low_ref, high_ref, gate_ref, out_ref):
    step, steps = pl.program_id(0), pl.num_programs(0)

    def write(ref):
        branch = own_ref[...] + ref[...].astype(jnp.float32)
        out_ref[...] = (gate_ref[...] * branch).astype(jnp.bfloat16)

    @pl.when(step < steps // 2)
    def _():
        write(low_ref)

    @pl.when(step >= steps // 2)
    def _():
        write(high_ref)


def combine(own, low, high, gate):
    rows, width = own.shape
    steps = 4
    each = width // steps
    column = pl.BlockSpec((rows, each), lambda n: (0, n))
    return pl.pallas_call(
        combine_kernel,
        grid=(steps,),
        in_specs=[
            column,
            pl.BlockSpec((rows, each), lambda n: (0, jnp.minimum(n, steps // 2 - 1))),
            pl.BlockSpec((rows, each), lambda n: (0, jnp.maximum(n - steps // 2, 0))),
            pl.BlockSpec((1, each), lambda n: (0, n)),
        ],
        out_specs=column,
        out_shape=jax.ShapeDtypeStruct((rows, width), jnp.bfloat16),
        compiler_params=params(),
        cost_estimate=cost(3 * rows * width, 10 * rows * width),
        name="combine",
    )(own, low, high, gate[None])


def local(
    hidden_in,
    shift_mod,
    scale_mod,
    gate_mod,
    w_qkv,
    norm_gain,
    w_out,
    spatial_mask,
    temporal_mask,
    frame_order,
):
    tokens = hidden_in.shape[1]
    pairs = w_qkv.shape[1]
    y, x, core, z = (lax.axis_index(name) for name in ("y", "x", "core", "frm"))
    chips = lax.axis_size("y") * lax.axis_size("x")
    planes = lax.axis_size("frm")
    chip = y * lax.axis_size("x") + x
    seq_index = chip * 2 + core

    def along_z(value, shift):
        return lax.ppermute(value, "frm", [(i, (i + shift) % planes) for i in range(planes)])

    def swap_cores(value):
        return lax.ppermute(value, "core", [(0, 1), (1, 0)])

    with jax.named_scope("modulate"):
        own = modulate(hidden_in[0], shift_mod, scale_mod)

    with jax.named_scope("gather_w_out"):
        turned = jnp.transpose(w_out, (0, 1, 3, 2))
        own, turned_far = lax.optimization_barrier((own, along_z(turned, 2)))
        out_weight = jnp.stack([turned, turned_far])
        out_weight = lax.all_gather(out_weight, ("y", "x", "core"), axis=0, tiled=False)

    with jax.named_scope("qkv"):
        weight = jnp.transpose(w_qkv, (1, 2, 0, 3))
        factor = jnp.array([LOG2E / math.sqrt(HD), 1.0], jnp.float32)
        norm_gain = jnp.transpose(norm_gain.reshape(pairs, 2, 2, HD), (1, 0, 2, 3))
        norm_gain = norm_gain * factor[None, None, :, None]
        after = along_z(own, -1)
        before = along_z(own, 1)
        spatial = heads([own], weight, norm_gain, 0, 4, 0)
        temporal = heads([own], weight, norm_gain, 1, pairs, 0)
        after, before, spatial, temporal = lax.optimization_barrier(
            (after, before, spatial, temporal)
        )
        cut = tokens // 2
        far = [along_z(before[:cut], 1), along_z(after[cut:], -1)]
        spatial = heads([after, before], weight, norm_gain, 0, 4, 2, spatial)
        temporal = heads([after, before], weight, norm_gain, 1, pairs, 2, temporal)
        far, spatial, temporal = lax.optimization_barrier((far, spatial, temporal))
        spatial = heads(far, weight, norm_gain, 0, 4, 1, spatial)
        spatial, far = lax.optimization_barrier((spatial, far))
        temporal = heads(far, weight, norm_gain, 1, pairs, 1, temporal)

    frames = (z + jnp.array(REL, jnp.int32)) % planes

    with jax.named_scope("temporal"):
        order = frame_order.astype(jnp.float32)[frames]
        distance = jnp.abs(order[:, None] - order[None, :])
        pair_global = (z * pairs + jnp.arange(pairs, dtype=jnp.int32)).astype(jnp.float32)
        slope = jnp.exp2(-(pair_global + 1.0) * 2.0 / HP)
        tmask = lax.dynamic_index_in_dim(temporal_mask, seq_index, 1, keepdims=False)
        tmask = tmask[:, frames][:, :, frames]
        bias_t = jnp.where(tmask > 0, -slope[:, None, None] * distance[None] * LOG2E, OFF)
        bias_t = jnp.repeat(bias_t, tokens, axis=2)[:, :, None, :]
        temporal_out = temporal_attention(temporal, bias_t)
        temporal_far = along_z(temporal_out[1:], 2)

    with jax.named_scope("spatial"):
        smask = lax.dynamic_index_in_dim(
            spatial_mask, jnp.minimum(x, pairs - 1), 0, keepdims=False
        )
        slot_frame = (z + jnp.array(REL, jnp.int32)[y]) % planes
        smask = lax.dynamic_index_in_dim(smask, slot_frame, 0, keepdims=False)
        smask = smask.reshape(chips, 2, chips, 2)
        smask = lax.dynamic_index_in_dim(smask, core, 1, keepdims=False)
        own_keys = lax.dynamic_index_in_dim(smask, core, 2, keepdims=False)
        other_keys = lax.dynamic_index_in_dim(smask, 1 - core, 2, keepdims=False)
        smask = jnp.concatenate([own_keys, other_keys], axis=1).T
        bias_s = jnp.where(smask > 0, 0.0, OFF).astype(jnp.float32)
        bias_s = jnp.pad(bias_s, ((0, 0), (0, HD - chips)))
        mine = lax.all_to_all(
            spatial.reshape(chips, tokens, 3 * HD), ("y", "x"), 0, 0, tiled=True
        )
        mine, temporal_out = lax.optimization_barrier((mine, temporal_out))
        other = swap_cores(mine)
        spatial_out = spatial_attention(mine, other, bias_s)
        spatial_out = lax.all_to_all(spatial_out, ("y", "x"), 0, 0, tiled=True)
        spatial_out = spatial_out.reshape(4, 4, tokens, HD)
        spatial_far = along_z(spatial_out[1:, :pairs], 2)

    with jax.named_scope("project"):
        partials = project(0, spatial_out, temporal_out, out_weight)
        kept, sent = project(1, spatial_far, temporal_far, out_weight, partials)
        half = sent.shape[1] // 2
        low = along_z(sent[:, :half], 1)
        high = along_z(sent[:, half:], -1)
        return combine(kept, low, high, gate_mod)[None]


def solution(mesh):
    split = Mesh(mesh.devices.reshape(4, 4, 2, 4), ("y", "x", "core", "frm"))
    seq = ("y", "x", "core")
    placed = (
        P("frm", seq, None),
        P(),
        P(),
        P(),
        P(None, "frm", None, None),
        P("frm", None, None),
        P("frm", None, None, seq),
        P("frm", None, None, None),
        P("frm", None, None, None),
        P(),
    )
    return jax.shard_map(
        local, mesh=split, in_specs=placed, out_specs=P("frm", seq, None), check_vma=False
    )
```

```python
import math

import jax
import jax.numpy as jnp
from jax import lax
from jax.experimental import pallas as pl
from jax.experimental.pallas import tpu as pltpu
from jax.sharding import Mesh, PartitionSpec as P

HP = 12
BLK = 128
HD = 128
EPS = 1e-06
LOG2E = 1.4426950408889634
OFF = -1e30
REL = (0, 2, 1, -1)
VMEM = 30 * 1024 * 1024
WIDE, NARROW = 40 * 1024 * 1024, 16 * 1024 * 1024


def params(limit=VMEM):
    return pltpu.CompilerParams(vmem_limit_bytes=limit)


def whole():
    return pl.BlockSpec(memory_space=pltpu.VMEM)


def cost(flops, size, trans=0):
    return pl.CostEstimate(flops=int(flops), bytes_accessed=int(size), transcendentals=int(trans))


def modulate_kernel(hidden_ref, shift_ref, scale_ref, low_ref, high_ref):
    rows = low_ref.shape[0]
    for at, out_ref in ((0, low_ref), (rows, high_ref)):
        values = hidden_ref[at : at + rows].astype(jnp.float32)
        centred = values - jnp.mean(values, axis=-1, keepdims=True)
        spread = jnp.mean(centred * centred, axis=-1, keepdims=True)
        out_ref[...] = (
            centred * lax.rsqrt(spread + EPS) * (1.0 + scale_ref[...]) + shift_ref[...]
        ).astype(jnp.bfloat16)


def modulate(hidden, shift_mod, scale_mod):
    rows, width = hidden.shape
    return pl.pallas_call(
        modulate_kernel,
        in_specs=[whole()] * 3,
        out_specs=[whole()] * 2,
        out_shape=[jax.ShapeDtypeStruct((rows // 2, width), jnp.bfloat16)] * 2,
        compiler_params=params(),
        cost_estimate=cost(10 * rows * width, 4 * rows * width),
        name="modulate",
    )(hidden, shift_mod[None], scale_mod[None])


def heads_kernel(parts, aliased, *refs):
    x_refs = refs[:parts]
    w_ref, gain_ref = refs[parts : parts + 2]
    out_ref, rows_ref = refs[parts + 2 + aliased :]
    pair = pl.program_id(0)
    frames, _, tokens, _ = out_ref.shape

    @pl.when(pair == 0)
    def _():
        at = 0
        for ref in x_refs:
            rows_ref[at : at + ref.shape[0], :] = ref[...]
            at += ref.shape[0]

    weight = jnp.concatenate([w_ref[0, j] for j in range(3)], axis=1)
    projected = jnp.dot(rows_ref[...], weight, preferred_element_type=jnp.float32)
    gains = gain_ref[pair]
    for j in range(3):
        v = projected[:, j * HD : (j + 1) * HD]
        if j < 2:
            square_mean = jnp.mean(v * v, axis=-1, keepdims=True)
            v = v * lax.rsqrt(square_mean + EPS) * gains[j : j + 1]
        out_ref[:, 0, :, j * HD : (j + 1) * HD] = v.astype(jnp.bfloat16).reshape(
            frames, tokens, HD
        )


def heads_both_kernel(parts, aliased, *refs):
    x_refs = refs[:parts]
    w_ref, gain_ref = refs[parts : parts + 2]
    spatial_ref, temporal_ref, rows_ref = refs[parts + 2 + aliased :]
    pair = pl.program_id(0)
    frames, _, tokens, _ = spatial_ref.shape

    @pl.when(pair == 0)
    def _():
        at = 0
        for ref in x_refs:
            rows_ref[at : at + ref.shape[0], :] = ref[...]
            at += ref.shape[0]

    weight = jnp.concatenate([w_ref[0, j] for j in range(6)], axis=1)
    projected = jnp.dot(rows_ref[...], weight, preferred_element_type=jnp.float32)
    for kind, out_ref in enumerate((spatial_ref, temporal_ref)):
        gains = gain_ref[kind, pair]
        for j in range(3):
            at = (kind * 3 + j) * HD
            v = projected[:, at : at + HD]
            if j < 2:
                square_mean = jnp.mean(v * v, axis=-1, keepdims=True)
                v = v * lax.rsqrt(square_mean + EPS) * gains[j : j + 1]
            out_ref[:, 0, :, j * HD : (j + 1) * HD] = v.astype(jnp.bfloat16).reshape(
                frames, tokens, HD
            )


def heads_both(pieces, weight, norm_gain, first, buffers=None):
    parts = len(pieces)
    width = pieces[0].shape[1]
    rows = sum(piece.shape[0] for piece in pieces)
    pairs = weight.shape[0]
    frames = rows // BLK
    triple = 3 * HD
    in_specs = [pl.BlockSpec(piece.shape, lambda n: (0, 0)) for piece in pieces]
    in_specs += [
        pl.BlockSpec((1, 6, width, HD), lambda n: (n, 0, 0, 0)),
        pl.BlockSpec((2, pairs, 2, HD), lambda n: (0, 0, 0, 0)),
    ]
    args = list(pieces) + [weight, norm_gain]
    aliases = {}
    if buffers is not None:
        in_specs += [pl.BlockSpec(memory_space=pl.ANY)] * 2
        aliases = {len(args): 0, len(args) + 1: 1}
        args += list(buffers)
    out_spec = pl.BlockSpec((frames, 1, BLK, triple), lambda n: (first // frames, n, 0, 0))
    return pl.pallas_call(
        lambda *refs: heads_both_kernel(parts, 2 * (buffers is not None), *refs),
        grid=(pairs,),
        in_specs=in_specs,
        out_specs=[out_spec, out_spec],
        out_shape=[
            jax.ShapeDtypeStruct((4, slots, BLK, triple), jnp.bfloat16) for slots in (4, pairs)
        ],
        scratch_shapes=[pltpu.VMEM((rows, width), jnp.bfloat16)],
        input_output_aliases=aliases,
        compiler_params=params(WIDE),
        cost_estimate=cost(4 * rows * width * pairs * triple, width * pairs * triple * 4),
        name="qkv_both",
    )(*args)


def heads(pieces, weight, norm_gain, kind, slots, first, buffer=None):
    parts = len(pieces)
    width = pieces[0].shape[1]
    rows = sum(piece.shape[0] for piece in pieces)
    pairs = weight.shape[0]
    block = kind if weight.shape[1] > 3 else 0
    frames = rows // BLK
    triple = 3 * HD
    aliased = buffer is not None
    in_specs = [pl.BlockSpec(piece.shape, lambda n: (0, 0)) for piece in pieces]
    in_specs += [
        pl.BlockSpec((1, 3, width, HD), lambda n: (n, block, 0, 0)),
        pl.BlockSpec((pairs, 2, HD), lambda n: (0, 0, 0)),
    ]
    args = list(pieces) + [weight, norm_gain[kind]]
    aliases = {}
    if aliased:
        in_specs.append(pl.BlockSpec(memory_space=pl.ANY))
        aliases = {len(args): 0}
        args.append(buffer)

    def body(*refs):
        heads_kernel(parts, int(aliased), *refs)

    return pl.pallas_call(
        body,
        grid=(pairs,),
        in_specs=in_specs,
        out_specs=pl.BlockSpec((frames, 1, BLK, triple), lambda n: (first // frames, n, 0, 0)),
        out_shape=jax.ShapeDtypeStruct((4, slots, BLK, triple), jnp.bfloat16),
        scratch_shapes=[pltpu.VMEM((rows, width), jnp.bfloat16)],
        input_output_aliases=aliases,
        compiler_params=params(),
        cost_estimate=cost(2 * rows * width * pairs * triple, width * pairs * triple * 2),
        name="qkv_spatial" if kind == 0 else "qkv_temporal",
    )(*args)


def spatial_kernel(own_ref, other_ref, bias_ref, out_ref):
    blocks = own_ref.shape[0]
    rows = blocks * BLK
    shape = (blocks, BLK, HD)
    one_hot = lax.broadcasted_iota(jnp.int32, shape, 2) == lax.broadcasted_iota(jnp.int32, shape, 0)
    one_hot = jnp.where(one_hot, 1.0, 0.0).astype(jnp.bfloat16)
    queries = jnp.concatenate([own_ref[:, :, 0:HD], one_hot], axis=2).reshape(rows, 2 * HD)
    per_chunk = 4
    chunk = per_chunk * BLK
    ones = jnp.ones((chunk, HD), jnp.bfloat16)
    summed = jnp.zeros((rows, 2 * HD), jnp.float32)
    for side, ref in enumerate((own_ref, other_ref)):
        for at in range(0, blocks, per_chunk):
            row = side * blocks + at
            bias = jnp.concatenate(
                [
                    jnp.broadcast_to(bias_ref[row + i : row + i + 1, :], (BLK, HD))
                    for i in range(per_chunk)
                ],
                axis=0,
            ).astype(jnp.bfloat16)
            keys = ref[at : at + per_chunk, :, HD : 2 * HD].reshape(chunk, HD)
            values = ref[at : at + per_chunk, :, 2 * HD :].reshape(chunk, HD)
            scores = lax.dot_general(
                queries, jnp.concatenate([keys, bias], axis=1), (((1,), (1,)), ((), ())),
                preferred_element_type=jnp.float32,
            )
            summed = summed + jnp.dot(
                jnp.exp2(scores).astype(jnp.bfloat16), jnp.concatenate([values, ones], axis=1),
                preferred_element_type=jnp.float32,
            )
    out_ref[...] = (summed[:, :HD] / summed[:, HD:]).astype(jnp.bfloat16).reshape(shape)


def spatial_attention(own, other, bias):
    blocks, tokens, triple = own.shape
    total = 2 * blocks * tokens
    return pl.pallas_call(
        spatial_kernel,
        in_specs=[whole()] * 3,
        out_specs=whole(),
        out_shape=jax.ShapeDtypeStruct((blocks, tokens, HD), jnp.bfloat16),
        compiler_params=params(),
        cost_estimate=cost(
            8 * blocks * tokens * total * HD, 4 * blocks * tokens * triple, blocks * tokens * total
        ),
        name="spatial_attention",
    )(own, other, bias)


def temporal_kernel(qkv_ref, bias_ref, out_ref):
    frames, _, tokens, _ = qkv_ref.shape
    rows = frames * tokens
    queries = qkv_ref[:, 0, :, 0:HD].reshape(rows, HD)
    keys = qkv_ref[:, 0, :, HD : 2 * HD].reshape(rows, HD)
    values = qkv_ref[:, 0, :, 2 * HD :].reshape(rows, HD)
    values = jnp.concatenate([values, jnp.ones((rows, HD), jnp.bfloat16)], axis=1)
    scores = lax.dot_general(
        queries, keys, (((1,), (1,)), ((), ())), preferred_element_type=jnp.float32
    )
    scores = scores.reshape(frames, tokens, rows) + bias_ref[0]
    weights = jnp.exp2(scores).astype(jnp.bfloat16).reshape(rows, rows)
    summed = jnp.dot(weights, values, preferred_element_type=jnp.float32)
    result = (summed[:, :HD] / summed[:, HD:]).astype(jnp.bfloat16)
    out_ref[:, 0] = result.reshape(frames, tokens, HD)


def temporal_attention(qkv, bias):
    frames, pairs, tokens, triple = qkv.shape
    rows = frames * tokens
    return pl.pallas_call(
        temporal_kernel,
        grid=(pairs,),
        in_specs=[
            pl.BlockSpec((frames, 1, tokens, triple), lambda h: (0, h, 0, 0)),
            pl.BlockSpec((1, frames, 1, rows), lambda h: (h, 0, 0, 0)),
        ],
        out_specs=pl.BlockSpec((frames, 1, tokens, HD), lambda h: (0, h, 0, 0)),
        out_shape=jax.ShapeDtypeStruct((frames, pairs, tokens, HD), jnp.bfloat16),
        compiler_params=params(),
        cost_estimate=cost(6 * pairs * rows * rows * HD, 2 * frames * pairs * tokens * triple),
        name="temporal_attention",
    )(qkv, bias)


OWN_SLOT = {0: 0, 1: 2, -1: 3}
FAR_SLOT = {0: 0, 1: 2, -1: 1}


def project_kernel(targets, groups, *refs):
    heads_count = 2 * len(groups)
    head_refs, w_ref = refs[:heads_count], refs[heads_count]
    rest, rows_ref = refs[heads_count + 1 : -1], refs[-1]
    step, steps = pl.program_id(0), pl.num_programs(0)
    shards, _, pairs, kinds, columns, _ = w_ref.shape
    depth = pairs * kinds * HD

    @pl.when(step == 0)
    def _():
        for number, target in enumerate(targets):
            for at_group, group in enumerate(groups):
                slot = (OWN_SLOT, FAR_SLOT)[group][target]
                for kind in range(kinds):
                    ref = head_refs[2 * at_group + kind]
                    for pair in range(pairs):
                        at = at_group * depth + (pair * kinds + kind) * HD
                        rows_ref[number, :, at : at + HD] = ref[slot, pair]

    weight = jnp.concatenate(
        [
            w_ref[:, at_group, pair, kind].reshape(shards * columns, HD)
            for at_group in range(len(groups))
            for pair in range(pairs)
            for kind in range(kinds)
        ],
        axis=1,
    )
    rows = rows_ref[step * len(targets) // steps]
    product = lax.dot_general(
        rows, weight, (((1,), (1,)), ((), ())), preferred_element_type=jnp.float32
    )
    if len(rest) == 1:
        rest[0][...] = product.astype(rest[0].dtype)
        return
    partial_ref, low_ref, high_ref = rest
    product = (product + partial_ref[...]).astype(jnp.bfloat16)

    @pl.when(step < steps // 2)
    def _():
        low_ref[...] = product

    @pl.when(step >= steps // 2)
    def _():
        high_ref[...] = product


def project(name, targets, groups, head_arrays, weight, dtype, limit, partial=None):
    shards, _, pairs, kinds, shard, _ = weight.shape
    per_step = 8
    steps, width = shards // per_step, per_step * shard
    depth = len(groups) * kinds * pairs * HD
    first = groups[0] // len(groups)
    column = pl.BlockSpec((BLK, width), lambda n: (0, n))
    partials = [] if partial is None else [partial]
    if partial is None:
        out_specs = column
        out_shape = jax.ShapeDtypeStruct((BLK, steps * width), dtype)
    else:
        out_specs = [
            pl.BlockSpec((BLK, width), lambda n: (0, jnp.minimum(n, steps // 2 - 1))),
            pl.BlockSpec((BLK, width), lambda n: (0, jnp.maximum(n - steps // 2, 0))),
        ]
        out_shape = [jax.ShapeDtypeStruct((BLK, steps // 2 * width), dtype)] * 2
    return pl.pallas_call(
        lambda *refs: project_kernel(targets, groups, *refs),
        grid=(steps,),
        in_specs=[pl.BlockSpec(array.shape, lambda n: (0, 0, 0, 0)) for array in head_arrays]
        + [
            pl.BlockSpec(
                (per_step, len(groups), pairs, kinds, shard, HD),
                lambda n: (n, first, 0, 0, 0, 0),
            )
        ]
        + [column] * len(partials),
        out_specs=out_specs,
        out_shape=out_shape,
        scratch_shapes=[pltpu.VMEM((len(targets), BLK, depth), jnp.bfloat16)],
        compiler_params=params(limit),
        cost_estimate=cost(2 * BLK * steps * width * depth, 2 * steps * width * depth),
        name=name,
    )(*head_arrays, weight, *partials)


def combine_kernel(own_ref, low_ref, high_ref, gate_ref, out_ref):
    step, steps = pl.program_id(0), pl.num_programs(0)

    def write(ref):
        branch = own_ref[...].astype(jnp.float32) + ref[...].astype(jnp.float32)
        out_ref[...] = (gate_ref[...] * branch).astype(jnp.bfloat16)

    @pl.when(step < steps // 2)
    def _():
        write(low_ref)

    @pl.when(step >= steps // 2)
    def _():
        write(high_ref)


def combine(own, low, high, gate):
    rows, width = own.shape
    steps = 2
    each = width // steps
    column = pl.BlockSpec((rows, each), lambda n: (0, n))
    return pl.pallas_call(
        combine_kernel,
        grid=(steps,),
        in_specs=[
            column,
            pl.BlockSpec((rows, each), lambda n: (0, jnp.minimum(n, steps // 2 - 1))),
            pl.BlockSpec((rows, each), lambda n: (0, jnp.maximum(n - steps // 2, 0))),
            pl.BlockSpec((1, each), lambda n: (0, n)),
        ],
        out_specs=column,
        out_shape=jax.ShapeDtypeStruct((rows, width), jnp.bfloat16),
        compiler_params=params(),
        cost_estimate=cost(3 * rows * width, 10 * rows * width),
        name="combine",
    )(own, low, high, gate[None])


def local(
    hidden_in,
    shift_mod,
    scale_mod,
    gate_mod,
    w_qkv,
    norm_gain,
    w_out,
    spatial_mask,
    temporal_mask,
    frame_order,
):
    tokens = hidden_in.shape[1]
    pairs = w_qkv.shape[1]
    y, x, core, z = (lax.axis_index(name) for name in ("y", "x", "core", "frm"))
    chips = lax.axis_size("y") * lax.axis_size("x")
    planes = lax.axis_size("frm")
    chip = y * lax.axis_size("x") + x
    seq_index = chip * 2 + core

    def along_z(value, shift):
        return lax.ppermute(value, "frm", [(i, (i + shift) % planes) for i in range(planes)])

    def swap_cores(value):
        return lax.ppermute(value, "core", [(0, 1), (1, 0)])

    with jax.named_scope("modulate"):
        own = modulate(hidden_in[0], shift_mod, scale_mod)

    with jax.named_scope("gather_w_out"):
        turned = jnp.transpose(w_out, (0, 1, 3, 2))
        low, high = own
        out_weight = jnp.stack([turned, along_z(turned, 2)])
        out_weight = lax.all_gather(out_weight, ("y", "x", "core"), axis=0, tiled=False)

    with jax.named_scope("qkv"):
        weight = jnp.transpose(w_qkv, (1, 2, 0, 3))
        factor = jnp.array([LOG2E / math.sqrt(HD), 1.0], jnp.float32)
        norm_gain = jnp.transpose(norm_gain.reshape(pairs, 2, 2, HD), (1, 0, 2, 3))
        norm_gain = norm_gain * factor[None, None, :, None]
        before_low, after_high = along_z(low, 1), along_z(high, -1)
        before_high, after_low = along_z(high, 1), along_z(low, -1)
        spatial, temporal = heads_both([low, high], weight, norm_gain, 0)
        before_low, after_high, spatial, temporal = lax.optimization_barrier(
            (before_low, after_high, spatial, temporal)
        )
        far = [along_z(before_low, 1), along_z(after_high, -1)]
        spatial, temporal = heads_both(
            [after_low, after_high, before_low, before_high],
            weight,
            norm_gain,
            2,
            (spatial, temporal),
        )
        far, spatial, temporal = lax.optimization_barrier((far, spatial, temporal))
        spatial = heads(far, weight, norm_gain, 0, 4, 1, spatial)
        spatial, far = lax.optimization_barrier((spatial, far))
        temporal = heads(far, weight, norm_gain, 1, pairs, 1, temporal)

    frames = (z + jnp.array(REL, jnp.int32)) % planes

    with jax.named_scope("temporal"):
        order = frame_order.astype(jnp.float32)[frames]
        distance = jnp.abs(order[:, None] - order[None, :])
        pair_global = (z * pairs + jnp.arange(pairs, dtype=jnp.int32)).astype(jnp.float32)
        slope = jnp.exp2(-(pair_global + 1.0) * 2.0 / HP)
        tmask = lax.dynamic_index_in_dim(temporal_mask, seq_index, 1, keepdims=False)
        tmask = tmask[:, frames][:, :, frames]
        bias_t = jnp.where(tmask > 0, -slope[:, None, None] * distance[None] * LOG2E, OFF)
        bias_t = jnp.repeat(bias_t, tokens, axis=2)[:, :, None, :]
        temporal_out = temporal_attention(temporal, bias_t)
        temporal_far = along_z(temporal_out[1:], 2)

    with jax.named_scope("spatial"):
        smask = lax.dynamic_index_in_dim(
            spatial_mask, jnp.minimum(x, pairs - 1), 0, keepdims=False
        )
        slot_frame = (z + jnp.array(REL, jnp.int32)[y]) % planes
        smask = lax.dynamic_index_in_dim(smask, slot_frame, 0, keepdims=False)
        smask = smask.reshape(chips, 2, chips, 2)
        smask = lax.dynamic_index_in_dim(smask, core, 1, keepdims=False)
        own_keys = lax.dynamic_index_in_dim(smask, core, 2, keepdims=False)
        other_keys = lax.dynamic_index_in_dim(smask, 1 - core, 2, keepdims=False)
        smask = jnp.concatenate([own_keys, other_keys], axis=1).T
        bias_s = jnp.where(smask > 0, 0.0, OFF).astype(jnp.float32)
        bias_s = jnp.pad(bias_s, ((0, 0), (0, HD - chips)))
        mine = lax.all_to_all(
            spatial.reshape(chips, tokens, 3 * HD), ("y", "x"), 0, 0, tiled=True
        )
        mine, temporal_out, bias_s, out_weight = lax.optimization_barrier(
            (mine, temporal_out, bias_s, out_weight)
        )
        other = swap_cores(mine)
        spatial_out = spatial_attention(mine, other, bias_s)
        spatial_out = lax.all_to_all(spatial_out, ("y", "x"), 0, 0, tiled=True)
        spatial_out = spatial_out.reshape(4, 4, tokens, HD)
        spatial_far = along_z(spatial_out[1:, :pairs], 2)

    with jax.named_scope("project"):
        own_heads, far_heads = [spatial_out, temporal_out], [spatial_far, temporal_far]
        sent = project(
            "project_sent_own_group", (1, -1), (0,), own_heads, out_weight, jnp.float32, WIDE
        )
        low, high = project(
            "project_sent", (1, -1), (1,), far_heads, out_weight, jnp.bfloat16, NARROW, sent
        )
        low = along_z(low, 1)
        high = along_z(high, -1)
        kept = project(
            "project_kept", (0,), (0, 1), own_heads + far_heads, out_weight, jnp.bfloat16, NARROW
        )
        return combine(kept, low, high, gate_mod)[None]


def solution(mesh):
    split = Mesh(mesh.devices.reshape(4, 4, 2, 4), ("y", "x", "core", "frm"))
    seq = ("y", "x", "core")
    placed = (
        P("frm", seq, None),
        P(),
        P(),
        P(),
        P(None, "frm", None, None),
        P("frm", None, None),
        P("frm", None, None, seq),
        P("frm", None, None, None),
        P("frm", None, None, None),
        P(),
    )
    return jax.shard_map(
        local, mesh=split, in_specs=placed, out_specs=P("frm", seq, None), check_vma=False
    )
```

```python
import math

import jax
import jax.numpy as jnp
from jax import lax
from jax.experimental import pallas as pl
from jax.experimental.pallas import tpu as pltpu
from jax.sharding import Mesh, PartitionSpec as P

HP = 12
BLK = 128
HD = 128
EPS = 1e-06
LOG2E = 1.4426950408889634
OFF = -1e30
REL = (0, 2, 1, -1)
VMEM = 30 * 1024 * 1024
WIDE, NARROW = 40 * 1024 * 1024, 16 * 1024 * 1024


def params(limit=VMEM):
    return pltpu.CompilerParams(vmem_limit_bytes=limit)


def whole():
    return pl.BlockSpec(memory_space=pltpu.VMEM)


def cost(flops, size, trans=0):
    return pl.CostEstimate(flops=int(flops), bytes_accessed=int(size), transcendentals=int(trans))


def modulate_kernel(hidden_ref, shift_ref, scale_ref, low_ref, high_ref):
    rows = low_ref.shape[0]
    for at, out_ref in ((0, low_ref), (rows, high_ref)):
        values = hidden_ref[at : at + rows].astype(jnp.float32)
        centred = values - jnp.mean(values, axis=-1, keepdims=True)
        spread = jnp.mean(centred * centred, axis=-1, keepdims=True)
        out_ref[...] = (
            centred * lax.rsqrt(spread + EPS) * (1.0 + scale_ref[...]) + shift_ref[...]
        ).astype(jnp.bfloat16)


def modulate(hidden, shift_mod, scale_mod):
    rows, width = hidden.shape
    return pl.pallas_call(
        modulate_kernel,
        in_specs=[whole()] * 3,
        out_specs=[whole()] * 2,
        out_shape=[jax.ShapeDtypeStruct((rows // 2, width), jnp.bfloat16)] * 2,
        compiler_params=params(),
        cost_estimate=cost(10 * rows * width, 4 * rows * width),
        name="modulate",
    )(hidden, shift_mod[None], scale_mod[None])


def heads_kernel(parts, aliased, *refs):
    x_refs = refs[:parts]
    w_ref, gain_ref = refs[parts : parts + 2]
    out_ref, rows_ref = refs[parts + 2 + aliased :]
    pair = pl.program_id(0)
    frames, _, tokens, _ = out_ref.shape

    @pl.when(pair == 0)
    def _():
        at = 0
        for ref in x_refs:
            rows_ref[at : at + ref.shape[0], :] = ref[...]
            at += ref.shape[0]

    weight = jnp.concatenate([w_ref[0, j] for j in range(3)], axis=1)
    projected = jnp.dot(rows_ref[...], weight, preferred_element_type=jnp.float32)
    gains = gain_ref[pair]
    for j in range(3):
        v = projected[:, j * HD : (j + 1) * HD]
        if j < 2:
            square_mean = jnp.mean(v * v, axis=-1, keepdims=True)
            v = v * lax.rsqrt(square_mean + EPS) * gains[j : j + 1]
        out_ref[:, 0, :, j * HD : (j + 1) * HD] = v.astype(jnp.bfloat16).reshape(
            frames, tokens, HD
        )


def heads_both_kernel(parts, aliased, *refs):
    x_refs = refs[:parts]
    w_ref, gain_ref = refs[parts : parts + 2]
    spatial_ref, temporal_ref, rows_ref = refs[parts + 2 + aliased :]
    pair = pl.program_id(0)
    frames, _, tokens, _ = spatial_ref.shape

    @pl.when(pair == 0)
    def _():
        at = 0
        for ref in x_refs:
            rows_ref[at : at + ref.shape[0], :] = ref[...]
            at += ref.shape[0]

    weight = jnp.concatenate([w_ref[0, j] for j in range(6)], axis=1)
    projected = jnp.dot(rows_ref[...], weight, preferred_element_type=jnp.float32)
    for kind, out_ref in enumerate((spatial_ref, temporal_ref)):
        gains = gain_ref[kind, pair]
        for j in range(3):
            at = (kind * 3 + j) * HD
            v = projected[:, at : at + HD]
            if j < 2:
                square_mean = jnp.mean(v * v, axis=-1, keepdims=True)
                v = v * lax.rsqrt(square_mean + EPS) * gains[j : j + 1]
            out_ref[:, 0, :, j * HD : (j + 1) * HD] = v.astype(jnp.bfloat16).reshape(
                frames, tokens, HD
            )


def heads_both(pieces, weight, norm_gain, first, buffers=None):
    parts = len(pieces)
    width = pieces[0].shape[1]
    rows = sum(piece.shape[0] for piece in pieces)
    pairs = weight.shape[0]
    frames = rows // BLK
    triple = 3 * HD
    in_specs = [pl.BlockSpec(piece.shape, lambda n: (0, 0)) for piece in pieces]
    in_specs += [
        pl.BlockSpec((1, 6, width, HD), lambda n: (n, 0, 0, 0)),
        pl.BlockSpec((2, pairs, 2, HD), lambda n: (0, 0, 0, 0)),
    ]
    args = list(pieces) + [weight, norm_gain]
    aliases = {}
    if buffers is not None:
        in_specs += [pl.BlockSpec(memory_space=pl.ANY)] * 2
        aliases = {len(args): 0, len(args) + 1: 1}
        args += list(buffers)
    out_spec = pl.BlockSpec((frames, 1, BLK, triple), lambda n: (first // frames, n, 0, 0))
    return pl.pallas_call(
        lambda *refs: heads_both_kernel(parts, 2 * (buffers is not None), *refs),
        grid=(pairs,),
        in_specs=in_specs,
        out_specs=[out_spec, out_spec],
        out_shape=[
            jax.ShapeDtypeStruct((4, slots, BLK, triple), jnp.bfloat16) for slots in (4, pairs)
        ],
        scratch_shapes=[pltpu.VMEM((rows, width), jnp.bfloat16)],
        input_output_aliases=aliases,
        compiler_params=params(WIDE),
        cost_estimate=cost(4 * rows * width * pairs * triple, width * pairs * triple * 4),
        name="qkv_both",
    )(*args)


def heads(pieces, weight, norm_gain, kind, slots, first, buffer=None):
    parts = len(pieces)
    width = pieces[0].shape[1]
    rows = sum(piece.shape[0] for piece in pieces)
    pairs = weight.shape[0]
    block = kind if weight.shape[1] > 3 else 0
    frames = rows // BLK
    triple = 3 * HD
    aliased = buffer is not None
    in_specs = [pl.BlockSpec(piece.shape, lambda n: (0, 0)) for piece in pieces]
    in_specs += [
        pl.BlockSpec((1, 3, width, HD), lambda n: (n, block, 0, 0)),
        pl.BlockSpec((pairs, 2, HD), lambda n: (0, 0, 0)),
    ]
    args = list(pieces) + [weight, norm_gain[kind]]
    aliases = {}
    if aliased:
        in_specs.append(pl.BlockSpec(memory_space=pl.ANY))
        aliases = {len(args): 0}
        args.append(buffer)

    def body(*refs):
        heads_kernel(parts, int(aliased), *refs)

    return pl.pallas_call(
        body,
        grid=(pairs,),
        in_specs=in_specs,
        out_specs=pl.BlockSpec((frames, 1, BLK, triple), lambda n: (first // frames, n, 0, 0)),
        out_shape=jax.ShapeDtypeStruct((4, slots, BLK, triple), jnp.bfloat16),
        scratch_shapes=[pltpu.VMEM((rows, width), jnp.bfloat16)],
        input_output_aliases=aliases,
        compiler_params=params(),
        cost_estimate=cost(2 * rows * width * pairs * triple, width * pairs * triple * 2),
        name="qkv_spatial" if kind == 0 else "qkv_temporal",
    )(*args)


def spatial_kernel(own_ref, other_ref, bias_ref, out_ref):
    blocks = own_ref.shape[0]
    rows = blocks * BLK
    shape = (blocks, BLK, HD)
    one_hot = lax.broadcasted_iota(jnp.int32, shape, 2) == lax.broadcasted_iota(jnp.int32, shape, 0)
    one_hot = jnp.where(one_hot, 1.0, 0.0).astype(jnp.bfloat16)
    queries = jnp.concatenate([own_ref[:, :, 0:HD], one_hot], axis=2).reshape(rows, 2 * HD)
    per_chunk = 4
    chunk = per_chunk * BLK
    ones = jnp.ones((chunk, HD), jnp.bfloat16)
    summed = jnp.zeros((rows, 2 * HD), jnp.float32)
    for side, ref in enumerate((own_ref, other_ref)):
        for at in range(0, blocks, per_chunk):
            row = side * blocks + at
            bias = jnp.concatenate(
                [
                    jnp.broadcast_to(bias_ref[row + i : row + i + 1, :], (BLK, HD))
                    for i in range(per_chunk)
                ],
                axis=0,
            ).astype(jnp.bfloat16)
            keys = ref[at : at + per_chunk, :, HD : 2 * HD].reshape(chunk, HD)
            values = ref[at : at + per_chunk, :, 2 * HD :].reshape(chunk, HD)
            scores = lax.dot_general(
                queries, jnp.concatenate([keys, bias], axis=1), (((1,), (1,)), ((), ())),
                preferred_element_type=jnp.float32,
            )
            summed = summed + jnp.dot(
                jnp.exp2(scores).astype(jnp.bfloat16), jnp.concatenate([values, ones], axis=1),
                preferred_element_type=jnp.float32,
            )
    out_ref[...] = (summed[:, :HD] / summed[:, HD:]).astype(jnp.bfloat16).reshape(shape)


def spatial_attention(own, other, bias):
    blocks, tokens, triple = own.shape
    total = 2 * blocks * tokens
    return pl.pallas_call(
        spatial_kernel,
        in_specs=[whole()] * 3,
        out_specs=whole(),
        out_shape=jax.ShapeDtypeStruct((blocks, tokens, HD), jnp.bfloat16),
        compiler_params=params(),
        cost_estimate=cost(
            8 * blocks * tokens * total * HD, 4 * blocks * tokens * triple, blocks * tokens * total
        ),
        name="spatial_attention",
    )(own, other, bias)


def temporal_kernel(qkv_ref, bias_ref, out_ref):
    frames, _, tokens, _ = qkv_ref.shape
    rows = frames * tokens
    queries = qkv_ref[:, 0, :, 0:HD].reshape(rows, HD)
    keys = qkv_ref[:, 0, :, HD : 2 * HD].reshape(rows, HD)
    values = qkv_ref[:, 0, :, 2 * HD :].reshape(rows, HD)
    values = jnp.concatenate([values, jnp.ones((rows, HD), jnp.bfloat16)], axis=1)
    scores = lax.dot_general(
        queries, keys, (((1,), (1,)), ((), ())), preferred_element_type=jnp.float32
    )
    scores = scores.reshape(frames, tokens, rows) + bias_ref[0]
    weights = jnp.exp2(scores).astype(jnp.bfloat16).reshape(rows, rows)
    summed = jnp.dot(weights, values, preferred_element_type=jnp.float32)
    result = (summed[:, :HD] / summed[:, HD:]).astype(jnp.bfloat16)
    out_ref[:, 0] = result.reshape(frames, tokens, HD)


def temporal_attention(qkv, bias):
    frames, pairs, tokens, triple = qkv.shape
    rows = frames * tokens
    return pl.pallas_call(
        temporal_kernel,
        grid=(pairs,),
        in_specs=[
            pl.BlockSpec((frames, 1, tokens, triple), lambda h: (0, h, 0, 0)),
            pl.BlockSpec((1, frames, 1, rows), lambda h: (h, 0, 0, 0)),
        ],
        out_specs=pl.BlockSpec((frames, 1, tokens, HD), lambda h: (0, h, 0, 0)),
        out_shape=jax.ShapeDtypeStruct((frames, pairs, tokens, HD), jnp.bfloat16),
        compiler_params=params(),
        cost_estimate=cost(6 * pairs * rows * rows * HD, 2 * frames * pairs * tokens * triple),
        name="temporal_attention",
    )(qkv, bias)


OWN_SLOT = {0: 0, 1: 2, -1: 3}
FAR_SLOT = {0: 0, 1: 2, -1: 1}


def project_kernel(targets, groups, *refs):
    heads_count = 2 * len(groups)
    head_refs, w_ref = refs[:heads_count], refs[heads_count]
    rest, rows_ref = refs[heads_count + 1 : -1], refs[-1]
    step, steps = pl.program_id(0), pl.num_programs(0)
    shards, _, pairs, kinds, columns, _ = w_ref.shape
    depth = pairs * kinds * HD

    @pl.when(step == 0)
    def _():
        for number, target in enumerate(targets):
            for at_group, group in enumerate(groups):
                slot = (OWN_SLOT, FAR_SLOT)[group][target]
                for kind in range(kinds):
                    ref = head_refs[2 * at_group + kind]
                    for pair in range(pairs):
                        at = at_group * depth + (pair * kinds + kind) * HD
                        rows_ref[number, :, at : at + HD] = ref[slot, pair]

    weight = jnp.concatenate(
        [
            w_ref[:, at_group, pair, kind].reshape(shards * columns, HD)
            for at_group in range(len(groups))
            for pair in range(pairs)
            for kind in range(kinds)
        ],
        axis=1,
    )
    rows = rows_ref[step * len(targets) // steps]
    product = lax.dot_general(
        rows, weight, (((1,), (1,)), ((), ())), preferred_element_type=jnp.float32
    )
    if len(rest) == 1:
        rest[0][...] = product.astype(rest[0].dtype)
        return
    partial_ref, low_ref, high_ref = rest
    product = (product + partial_ref[...]).astype(jnp.bfloat16)

    @pl.when(step < steps // 2)
    def _():
        low_ref[...] = product

    @pl.when(step >= steps // 2)
    def _():
        high_ref[...] = product


def project(name, targets, groups, head_arrays, weight, dtype, limit, partial=None):
    shards, _, pairs, kinds, shard, _ = weight.shape
    per_step = 8
    steps, width = shards // per_step, per_step * shard
    depth = len(groups) * kinds * pairs * HD
    first = groups[0] // len(groups)
    column = pl.BlockSpec((BLK, width), lambda n: (0, n))
    partials = [] if partial is None else [partial]
    if partial is None:
        out_specs = column
        out_shape = jax.ShapeDtypeStruct((BLK, steps * width), dtype)
    else:
        out_specs = [
            pl.BlockSpec((BLK, width), lambda n: (0, jnp.minimum(n, steps // 2 - 1))),
            pl.BlockSpec((BLK, width), lambda n: (0, jnp.maximum(n - steps // 2, 0))),
        ]
        out_shape = [jax.ShapeDtypeStruct((BLK, steps // 2 * width), dtype)] * 2
    return pl.pallas_call(
        lambda *refs: project_kernel(targets, groups, *refs),
        grid=(steps,),
        in_specs=[pl.BlockSpec(array.shape, lambda n: (0, 0, 0, 0)) for array in head_arrays]
        + [
            pl.BlockSpec(
                (per_step, len(groups), pairs, kinds, shard, HD),
                lambda n: (n, first, 0, 0, 0, 0),
            )
        ]
        + [column] * len(partials),
        out_specs=out_specs,
        out_shape=out_shape,
        scratch_shapes=[pltpu.VMEM((len(targets), BLK, depth), jnp.bfloat16)],
        compiler_params=params(limit),
        cost_estimate=cost(2 * BLK * steps * width * depth, 2 * steps * width * depth),
        name=name,
    )(*head_arrays, weight, *partials)


def combine_kernel(own_ref, low_ref, high_ref, gate_ref, out_ref):
    step, steps = pl.program_id(0), pl.num_programs(0)

    def write(ref):
        branch = own_ref[...].astype(jnp.float32) + ref[...].astype(jnp.float32)
        out_ref[...] = (gate_ref[...] * branch).astype(jnp.bfloat16)

    @pl.when(step < steps // 2)
    def _():
        write(low_ref)

    @pl.when(step >= steps // 2)
    def _():
        write(high_ref)


def combine(own, low, high, gate):
    rows, width = own.shape
    steps = 2
    each = width // steps
    column = pl.BlockSpec((rows, each), lambda n: (0, n))
    return pl.pallas_call(
        combine_kernel,
        grid=(steps,),
        in_specs=[
            column,
            pl.BlockSpec((rows, each), lambda n: (0, jnp.minimum(n, steps // 2 - 1))),
            pl.BlockSpec((rows, each), lambda n: (0, jnp.maximum(n - steps // 2, 0))),
            pl.BlockSpec((1, each), lambda n: (0, n)),
        ],
        out_specs=column,
        out_shape=jax.ShapeDtypeStruct((rows, width), jnp.bfloat16),
        compiler_params=params(),
        cost_estimate=cost(3 * rows * width, 10 * rows * width),
        name="combine",
    )(own, low, high, gate[None])


def local(
    hidden_in,
    shift_mod,
    scale_mod,
    gate_mod,
    w_qkv,
    norm_gain,
    w_out,
    spatial_mask,
    temporal_mask,
    frame_order,
):
    tokens = hidden_in.shape[1]
    pairs = w_qkv.shape[1]
    y, x, core, z = (lax.axis_index(name) for name in ("y", "x", "core", "frm"))
    chips = lax.axis_size("y") * lax.axis_size("x")
    planes = lax.axis_size("frm")
    chip = y * lax.axis_size("x") + x
    seq_index = chip * 2 + core

    def along_z(value, shift):
        return lax.ppermute(value, "frm", [(i, (i + shift) % planes) for i in range(planes)])

    def swap_cores(value):
        return lax.ppermute(value, "core", [(0, 1), (1, 0)])

    with jax.named_scope("modulate"):
        own = modulate(hidden_in[0], shift_mod, scale_mod)

    with jax.named_scope("gather_w_out"):
        turned = jnp.transpose(w_out, (0, 1, 3, 2))
        (low, high), turned_far = lax.optimization_barrier((own, along_z(turned, 2)))
        out_weight = jnp.stack([turned, turned_far])
        out_weight = lax.all_gather(out_weight, ("y", "x", "core"), axis=0, tiled=False)

    with jax.named_scope("qkv"):
        weight = jnp.transpose(w_qkv, (1, 2, 0, 3))
        factor = jnp.array([LOG2E / math.sqrt(HD), 1.0], jnp.float32)
        norm_gain = jnp.transpose(norm_gain.reshape(pairs, 2, 2, HD), (1, 0, 2, 3))
        norm_gain = norm_gain * factor[None, None, :, None]
        before_low, after_high = along_z(low, 1), along_z(high, -1)
        before_high, after_low = along_z(high, 1), along_z(low, -1)
        spatial, temporal = heads_both([low, high], weight, norm_gain, 0)
        before_low, after_high, spatial, temporal = lax.optimization_barrier(
            (before_low, after_high, spatial, temporal)
        )
        far = [along_z(before_low, 1), along_z(after_high, -1)]
        spatial, temporal = heads_both(
            [after_low, after_high, before_low, before_high],
            weight,
            norm_gain,
            2,
            (spatial, temporal),
        )
        far, spatial, temporal = lax.optimization_barrier((far, spatial, temporal))
        spatial = heads(far, weight, norm_gain, 0, 4, 1, spatial)
        spatial, far = lax.optimization_barrier((spatial, far))
        temporal = heads(far, weight, norm_gain, 1, pairs, 1, temporal)

    frames = (z + jnp.array(REL, jnp.int32)) % planes

    with jax.named_scope("temporal"):
        order = frame_order.astype(jnp.float32)[frames]
        distance = jnp.abs(order[:, None] - order[None, :])
        pair_global = (z * pairs + jnp.arange(pairs, dtype=jnp.int32)).astype(jnp.float32)
        slope = jnp.exp2(-(pair_global + 1.0) * 2.0 / HP)
        tmask = lax.dynamic_index_in_dim(temporal_mask, seq_index, 1, keepdims=False)
        tmask = tmask[:, frames][:, :, frames]
        bias_t = jnp.where(tmask > 0, -slope[:, None, None] * distance[None] * LOG2E, OFF)
        bias_t = jnp.repeat(bias_t, tokens, axis=2)[:, :, None, :]
        temporal_out = temporal_attention(temporal, bias_t)
        temporal_far = along_z(temporal_out[1:], 2)

    with jax.named_scope("spatial"):
        smask = lax.dynamic_index_in_dim(
            spatial_mask, jnp.minimum(x, pairs - 1), 0, keepdims=False
        )
        slot_frame = (z + jnp.array(REL, jnp.int32)[y]) % planes
        smask = lax.dynamic_index_in_dim(smask, slot_frame, 0, keepdims=False)
        smask = smask.reshape(chips, 2, chips, 2)
        smask = lax.dynamic_index_in_dim(smask, core, 1, keepdims=False)
        own_keys = lax.dynamic_index_in_dim(smask, core, 2, keepdims=False)
        other_keys = lax.dynamic_index_in_dim(smask, 1 - core, 2, keepdims=False)
        smask = jnp.concatenate([own_keys, other_keys], axis=1).T
        bias_s = jnp.where(smask > 0, 0.0, OFF).astype(jnp.float32)
        bias_s = jnp.pad(bias_s, ((0, 0), (0, HD - chips)))
        mine = lax.all_to_all(
            spatial.reshape(chips, tokens, 3 * HD), ("y", "x"), 0, 0, tiled=True
        )
        mine, temporal_out, temporal_far, bias_s, out_weight = lax.optimization_barrier(
            (mine, temporal_out, temporal_far, bias_s, out_weight)
        )
        other = swap_cores(mine)
        spatial_out = spatial_attention(mine, other, bias_s)
        spatial_out = lax.all_to_all(spatial_out, ("y", "x"), 0, 0, tiled=True)
        spatial_out = spatial_out.reshape(4, 4, tokens, HD)
        spatial_far = along_z(spatial_out[1:, :pairs], 2)

    with jax.named_scope("project"):
        own_heads, far_heads = [spatial_out, temporal_out], [spatial_far, temporal_far]
        sent = project(
            "project_sent_own_group", (1, -1), (0,), own_heads, out_weight, jnp.float32, WIDE
        )
        low, high = project(
            "project_sent", (1, -1), (1,), far_heads, out_weight, jnp.bfloat16, NARROW, sent
        )
        low = along_z(low, 1)
        high = along_z(high, -1)
        kept = project(
            "project_kept", (0,), (0, 1), own_heads + far_heads, out_weight, jnp.bfloat16, NARROW
        )
        return combine(kept, low, high, gate_mod)[None]


def solution(mesh):
    split = Mesh(mesh.devices.reshape(4, 4, 2, 4), ("y", "x", "core", "frm"))
    seq = ("y", "x", "core")
    placed = (
        P("frm", seq, None),
        P(),
        P(),
        P(),
        P(None, "frm", None, None),
        P("frm", None, None),
        P("frm", None, None, seq),
        P("frm", None, None, None),
        P("frm", None, None, None),
        P(),
    )
    return jax.shard_map(
        local, mesh=split, in_specs=placed, out_specs=P("frm", seq, None), check_vma=False
    )
```

```python
import math

import jax
import jax.numpy as jnp
from jax import lax
from jax.experimental import pallas as pl
from jax.experimental.pallas import tpu as pltpu
from jax.sharding import Mesh, PartitionSpec as P

HP = 12
BLK = 128
HD = 128
EPS = 1e-06
LOG2E = 1.4426950408889634
OFF = -1e30
REL = (0, 2, 1, -1)
VMEM = 30 * 1024 * 1024
WIDE, NARROW = 40 * 1024 * 1024, 16 * 1024 * 1024


def params(limit=VMEM):
    return pltpu.CompilerParams(vmem_limit_bytes=limit)


def whole():
    return pl.BlockSpec(memory_space=pltpu.VMEM)


def cost(flops, size, trans=0):
    return pl.CostEstimate(flops=int(flops), bytes_accessed=int(size), transcendentals=int(trans))


def modulate_kernel(hidden_ref, shift_ref, scale_ref, low_ref, high_ref):
    rows = low_ref.shape[0]
    for at, out_ref in ((0, low_ref), (rows, high_ref)):
        values = hidden_ref[at : at + rows].astype(jnp.float32)
        centred = values - jnp.mean(values, axis=-1, keepdims=True)
        spread = jnp.mean(centred * centred, axis=-1, keepdims=True)
        out_ref[...] = (
            centred * lax.rsqrt(spread + EPS) * (1.0 + scale_ref[...]) + shift_ref[...]
        ).astype(jnp.bfloat16)


def modulate(hidden, shift_mod, scale_mod):
    rows, width = hidden.shape
    return pl.pallas_call(
        modulate_kernel,
        in_specs=[whole()] * 3,
        out_specs=[whole()] * 2,
        out_shape=[jax.ShapeDtypeStruct((rows // 2, width), jnp.bfloat16)] * 2,
        compiler_params=params(),
        cost_estimate=cost(10 * rows * width, 4 * rows * width),
        name="modulate",
    )(hidden, shift_mod[None], scale_mod[None])


def heads_kernel(parts, aliased, *refs):
    x_refs = refs[:parts]
    w_ref, gain_ref = refs[parts : parts + 2]
    out_ref, rows_ref = refs[parts + 2 + aliased :]
    pair = pl.program_id(0)
    frames, _, tokens, _ = out_ref.shape

    @pl.when(pair == 0)
    def _():
        at = 0
        for ref in x_refs:
            rows_ref[at : at + ref.shape[0], :] = ref[...]
            at += ref.shape[0]

    weight = jnp.concatenate([w_ref[0, j] for j in range(3)], axis=1)
    projected = jnp.dot(rows_ref[...], weight, preferred_element_type=jnp.float32)
    gains = gain_ref[pair]
    for j in range(3):
        v = projected[:, j * HD : (j + 1) * HD]
        if j < 2:
            square_mean = jnp.mean(v * v, axis=-1, keepdims=True)
            v = v * lax.rsqrt(square_mean + EPS) * gains[j : j + 1]
        out_ref[:, 0, :, j * HD : (j + 1) * HD] = v.astype(jnp.bfloat16).reshape(
            frames, tokens, HD
        )


def heads_both_kernel(parts, aliased, *refs):
    x_refs = refs[:parts]
    w_ref, gain_ref = refs[parts : parts + 2]
    spatial_ref, temporal_ref, rows_ref = refs[parts + 2 + aliased :]
    pair = pl.program_id(0)
    frames, _, tokens, _ = spatial_ref.shape

    @pl.when(pair == 0)
    def _():
        at = 0
        for ref in x_refs:
            rows_ref[at : at + ref.shape[0], :] = ref[...]
            at += ref.shape[0]

    weight = jnp.concatenate([w_ref[0, j] for j in range(6)], axis=1)
    projected = jnp.dot(rows_ref[...], weight, preferred_element_type=jnp.float32)
    for kind, out_ref in enumerate((spatial_ref, temporal_ref)):
        gains = gain_ref[kind, pair]
        for j in range(3):
            at = (kind * 3 + j) * HD
            v = projected[:, at : at + HD]
            if j < 2:
                square_mean = jnp.mean(v * v, axis=-1, keepdims=True)
                v = v * lax.rsqrt(square_mean + EPS) * gains[j : j + 1]
            out_ref[:, 0, :, j * HD : (j + 1) * HD] = v.astype(jnp.bfloat16).reshape(
                frames, tokens, HD
            )


def heads_both(pieces, weight, norm_gain, first, buffers=None):
    parts = len(pieces)
    width = pieces[0].shape[1]
    rows = sum(piece.shape[0] for piece in pieces)
    pairs = weight.shape[0]
    frames = rows // BLK
    triple = 3 * HD
    in_specs = [pl.BlockSpec(piece.shape, lambda n: (0, 0)) for piece in pieces]
    in_specs += [
        pl.BlockSpec((1, 6, width, HD), lambda n: (n, 0, 0, 0)),
        pl.BlockSpec((2, pairs, 2, HD), lambda n: (0, 0, 0, 0)),
    ]
    args = list(pieces) + [weight, norm_gain]
    aliases = {}
    if buffers is not None:
        in_specs += [pl.BlockSpec(memory_space=pl.ANY)] * 2
        aliases = {len(args): 0, len(args) + 1: 1}
        args += list(buffers)
    out_spec = pl.BlockSpec((frames, 1, BLK, triple), lambda n: (first // frames, n, 0, 0))
    return pl.pallas_call(
        lambda *refs: heads_both_kernel(parts, 2 * (buffers is not None), *refs),
        grid=(pairs,),
        in_specs=in_specs,
        out_specs=[out_spec, out_spec],
        out_shape=[
            jax.ShapeDtypeStruct((4, slots, BLK, triple), jnp.bfloat16) for slots in (4, pairs)
        ],
        scratch_shapes=[pltpu.VMEM((rows, width), jnp.bfloat16)],
        input_output_aliases=aliases,
        compiler_params=params(WIDE),
        cost_estimate=cost(4 * rows * width * pairs * triple, width * pairs * triple * 4),
        name="qkv_both",
    )(*args)


def heads(pieces, weight, norm_gain, kind, slots, first, buffer=None):
    parts = len(pieces)
    width = pieces[0].shape[1]
    rows = sum(piece.shape[0] for piece in pieces)
    pairs = weight.shape[0]
    block = kind if weight.shape[1] > 3 else 0
    frames = rows // BLK
    triple = 3 * HD
    aliased = buffer is not None
    in_specs = [pl.BlockSpec(piece.shape, lambda n: (0, 0)) for piece in pieces]
    in_specs += [
        pl.BlockSpec((1, 3, width, HD), lambda n: (n, block, 0, 0)),
        pl.BlockSpec((pairs, 2, HD), lambda n: (0, 0, 0)),
    ]
    args = list(pieces) + [weight, norm_gain[kind]]
    aliases = {}
    if aliased:
        in_specs.append(pl.BlockSpec(memory_space=pl.ANY))
        aliases = {len(args): 0}
        args.append(buffer)

    def body(*refs):
        heads_kernel(parts, int(aliased), *refs)

    return pl.pallas_call(
        body,
        grid=(pairs,),
        in_specs=in_specs,
        out_specs=pl.BlockSpec((frames, 1, BLK, triple), lambda n: (first // frames, n, 0, 0)),
        out_shape=jax.ShapeDtypeStruct((4, slots, BLK, triple), jnp.bfloat16),
        scratch_shapes=[pltpu.VMEM((rows, width), jnp.bfloat16)],
        input_output_aliases=aliases,
        compiler_params=params(),
        cost_estimate=cost(2 * rows * width * pairs * triple, width * pairs * triple * 2),
        name="qkv_spatial" if kind == 0 else "qkv_temporal",
    )(*args)


def spatial_kernel(side, own_ref, keys_ref, bias_ref, *refs):
    blocks = own_ref.shape[0]
    rows = blocks * BLK
    shape = (blocks, BLK, HD)
    one_hot = lax.broadcasted_iota(jnp.int32, shape, 2) == lax.broadcasted_iota(jnp.int32, shape, 0)
    one_hot = jnp.where(one_hot, 1.0, 0.0).astype(jnp.bfloat16)
    queries = jnp.concatenate([own_ref[:, :, 0:HD], one_hot], axis=2).reshape(rows, 2 * HD)
    per_chunk = 4
    chunk = per_chunk * BLK
    ones = jnp.ones((chunk, HD), jnp.bfloat16)
    out_ref = refs[-1]
    summed = jnp.zeros((rows, 2 * HD), jnp.float32) if side == 0 else refs[0][...]
    for ref in (keys_ref,):
        for at in range(0, blocks, per_chunk):
            row = side * blocks + at
            bias = jnp.concatenate(
                [
                    jnp.broadcast_to(bias_ref[row + i : row + i + 1, :], (BLK, HD))
                    for i in range(per_chunk)
                ],
                axis=0,
            ).astype(jnp.bfloat16)
            keys = ref[at : at + per_chunk, :, HD : 2 * HD].reshape(chunk, HD)
            values = ref[at : at + per_chunk, :, 2 * HD :].reshape(chunk, HD)
            scores = lax.dot_general(
                queries, jnp.concatenate([keys, bias], axis=1), (((1,), (1,)), ((), ())),
                preferred_element_type=jnp.float32,
            )
            summed = summed + jnp.dot(
                jnp.exp2(scores).astype(jnp.bfloat16), jnp.concatenate([values, ones], axis=1),
                preferred_element_type=jnp.float32,
            )
    if side == 0:
        out_ref[...] = summed
        return
    out_ref[...] = (summed[:, :HD] / summed[:, HD:]).astype(jnp.bfloat16).reshape(shape)


def spatial_attention(own, keys, bias, partial=None):
    blocks, tokens, triple = own.shape
    rows = blocks * tokens
    side = 0 if partial is None else 1
    args = [own, keys, bias] + ([] if partial is None else [partial])
    out = ((rows, 2 * HD), jnp.float32) if side == 0 else ((blocks, tokens, HD), jnp.bfloat16)
    return pl.pallas_call(
        lambda *refs: spatial_kernel(side, *refs),
        in_specs=[whole()] * len(args),
        out_specs=whole(),
        out_shape=jax.ShapeDtypeStruct(*out),
        compiler_params=params(),
        cost_estimate=cost(8 * rows * rows * HD, 4 * rows * triple, rows * rows),
        name=("spatial_attention_own", "spatial_attention_other")[side],
    )(*args)


def temporal_kernel(qkv_ref, bias_ref, out_ref):
    frames, _, tokens, _ = qkv_ref.shape
    rows = frames * tokens
    queries = qkv_ref[:, 0, :, 0:HD].reshape(rows, HD)
    keys = qkv_ref[:, 0, :, HD : 2 * HD].reshape(rows, HD)
    values = qkv_ref[:, 0, :, 2 * HD :].reshape(rows, HD)
    values = jnp.concatenate([values, jnp.ones((rows, HD), jnp.bfloat16)], axis=1)
    scores = lax.dot_general(
        queries, keys, (((1,), (1,)), ((), ())), preferred_element_type=jnp.float32
    )
    scores = scores.reshape(frames, tokens, rows) + bias_ref[0]
    weights = jnp.exp2(scores).astype(jnp.bfloat16).reshape(rows, rows)
    summed = jnp.dot(weights, values, preferred_element_type=jnp.float32)
    result = (summed[:, :HD] / summed[:, HD:]).astype(jnp.bfloat16)
    out_ref[:, 0] = result.reshape(frames, tokens, HD)


def temporal_attention(qkv, bias):
    frames, pairs, tokens, triple = qkv.shape
    rows = frames * tokens
    return pl.pallas_call(
        temporal_kernel,
        grid=(pairs,),
        in_specs=[
            pl.BlockSpec((frames, 1, tokens, triple), lambda h: (0, h, 0, 0)),
            pl.BlockSpec((1, frames, 1, rows), lambda h: (h, 0, 0, 0)),
        ],
        out_specs=pl.BlockSpec((frames, 1, tokens, HD), lambda h: (0, h, 0, 0)),
        out_shape=jax.ShapeDtypeStruct((frames, pairs, tokens, HD), jnp.bfloat16),
        compiler_params=params(),
        cost_estimate=cost(6 * pairs * rows * rows * HD, 2 * frames * pairs * tokens * triple),
        name="temporal_attention",
    )(qkv, bias)


OWN_SLOT = {0: 0, 1: 2, -1: 3}
FAR_SLOT = {0: 0, 1: 2, -1: 1}


def project_kernel(targets, groups, *refs):
    heads_count = 2 * len(groups)
    head_refs, w_ref = refs[:heads_count], refs[heads_count]
    rest, rows_ref = refs[heads_count + 1 : -1], refs[-1]
    step, steps = pl.program_id(0), pl.num_programs(0)
    shards, _, pairs, kinds, columns, _ = w_ref.shape
    depth = pairs * kinds * HD

    @pl.when(step == 0)
    def _():
        for number, target in enumerate(targets):
            for at_group, group in enumerate(groups):
                slot = (OWN_SLOT, FAR_SLOT)[group][target]
                for kind in range(kinds):
                    ref = head_refs[2 * at_group + kind]
                    for pair in range(pairs):
                        at = at_group * depth + (pair * kinds + kind) * HD
                        rows_ref[number, :, at : at + HD] = ref[slot, pair]

    weight = jnp.concatenate(
        [
            w_ref[:, at_group, pair, kind].reshape(shards * columns, HD)
            for at_group in range(len(groups))
            for pair in range(pairs)
            for kind in range(kinds)
        ],
        axis=1,
    )
    rows = rows_ref[step * len(targets) // steps]
    product = lax.dot_general(
        rows, weight, (((1,), (1,)), ((), ())), preferred_element_type=jnp.float32
    )
    if len(rest) == 1:
        rest[0][...] = product.astype(rest[0].dtype)
        return
    partial_ref, low_ref, high_ref = rest
    product = (product + partial_ref[...]).astype(jnp.bfloat16)

    @pl.when(step < steps // 2)
    def _():
        low_ref[...] = product

    @pl.when(step >= steps // 2)
    def _():
        high_ref[...] = product


def project(name, targets, groups, head_arrays, weight, dtype, limit, partial=None):
    shards, _, pairs, kinds, shard, _ = weight.shape
    per_step = 8
    steps, width = shards // per_step, per_step * shard
    depth = len(groups) * kinds * pairs * HD
    first = groups[0] // len(groups)
    column = pl.BlockSpec((BLK, width), lambda n: (0, n))
    partials = [] if partial is None else [partial]
    if partial is None:
        out_specs = column
        out_shape = jax.ShapeDtypeStruct((BLK, steps * width), dtype)
    else:
        out_specs = [
            pl.BlockSpec((BLK, width), lambda n: (0, jnp.minimum(n, steps // 2 - 1))),
            pl.BlockSpec((BLK, width), lambda n: (0, jnp.maximum(n - steps // 2, 0))),
        ]
        out_shape = [jax.ShapeDtypeStruct((BLK, steps // 2 * width), dtype)] * 2
    return pl.pallas_call(
        lambda *refs: project_kernel(targets, groups, *refs),
        grid=(steps,),
        in_specs=[pl.BlockSpec(array.shape, lambda n: (0, 0, 0, 0)) for array in head_arrays]
        + [
            pl.BlockSpec(
                (per_step, len(groups), pairs, kinds, shard, HD),
                lambda n: (n, first, 0, 0, 0, 0),
            )
        ]
        + [column] * len(partials),
        out_specs=out_specs,
        out_shape=out_shape,
        scratch_shapes=[pltpu.VMEM((len(targets), BLK, depth), jnp.bfloat16)],
        compiler_params=params(limit),
        cost_estimate=cost(2 * BLK * steps * width * depth, 2 * steps * width * depth),
        name=name,
    )(*head_arrays, weight, *partials)


def combine_kernel(own_ref, low_ref, high_ref, gate_ref, out_ref):
    step, steps = pl.program_id(0), pl.num_programs(0)

    def write(ref):
        branch = own_ref[...].astype(jnp.float32) + ref[...].astype(jnp.float32)
        out_ref[...] = (gate_ref[...] * branch).astype(jnp.bfloat16)

    @pl.when(step < steps // 2)
    def _():
        write(low_ref)

    @pl.when(step >= steps // 2)
    def _():
        write(high_ref)


def combine(own, low, high, gate):
    rows, width = own.shape
    steps = 2
    each = width // steps
    column = pl.BlockSpec((rows, each), lambda n: (0, n))
    return pl.pallas_call(
        combine_kernel,
        grid=(steps,),
        in_specs=[
            column,
            pl.BlockSpec((rows, each), lambda n: (0, jnp.minimum(n, steps // 2 - 1))),
            pl.BlockSpec((rows, each), lambda n: (0, jnp.maximum(n - steps // 2, 0))),
            pl.BlockSpec((1, each), lambda n: (0, n)),
        ],
        out_specs=column,
        out_shape=jax.ShapeDtypeStruct((rows, width), jnp.bfloat16),
        compiler_params=params(),
        cost_estimate=cost(3 * rows * width, 10 * rows * width),
        name="combine",
    )(own, low, high, gate[None])


def local(
    hidden_in,
    shift_mod,
    scale_mod,
    gate_mod,
    w_qkv,
    norm_gain,
    w_out,
    spatial_mask,
    temporal_mask,
    frame_order,
):
    tokens = hidden_in.shape[1]
    pairs = w_qkv.shape[1]
    y, x, core, z = (lax.axis_index(name) for name in ("y", "x", "core", "frm"))
    chips = lax.axis_size("y") * lax.axis_size("x")
    planes = lax.axis_size("frm")
    chip = y * lax.axis_size("x") + x
    seq_index = chip * 2 + core

    def along_z(value, shift):
        return lax.ppermute(value, "frm", [(i, (i + shift) % planes) for i in range(planes)])

    def swap_cores(value):
        return lax.ppermute(value, "core", [(0, 1), (1, 0)])

    with jax.named_scope("modulate"):
        own = modulate(hidden_in[0], shift_mod, scale_mod)

    with jax.named_scope("gather_w_out"):
        turned = jnp.transpose(w_out, (0, 1, 3, 2))
        (low, high), turned_far = lax.optimization_barrier((own, along_z(turned, 2)))
        out_weight = jnp.stack([turned, turned_far])
        out_weight = lax.all_gather(out_weight, ("y", "x", "core"), axis=0, tiled=False)

    with jax.named_scope("qkv"):
        weight = jnp.transpose(w_qkv, (1, 2, 0, 3))
        factor = jnp.array([LOG2E / math.sqrt(HD), 1.0], jnp.float32)
        norm_gain = jnp.transpose(norm_gain.reshape(pairs, 2, 2, HD), (1, 0, 2, 3))
        norm_gain = norm_gain * factor[None, None, :, None]
        before_low, after_high = along_z(low, 1), along_z(high, -1)
        before_high, after_low = along_z(high, 1), along_z(low, -1)
        spatial, temporal = heads_both([low, high], weight, norm_gain, 0)
        before_low, after_high, spatial, temporal = lax.optimization_barrier(
            (before_low, after_high, spatial, temporal)
        )
        far = [along_z(before_low, 1), along_z(after_high, -1)]
        spatial, temporal = heads_both(
            [after_low, after_high, before_low, before_high],
            weight,
            norm_gain,
            2,
            (spatial, temporal),
        )
        far, spatial, temporal = lax.optimization_barrier((far, spatial, temporal))
        spatial = heads(far, weight, norm_gain, 0, 4, 1, spatial)
        spatial, far = lax.optimization_barrier((spatial, far))
        temporal = heads(far, weight, norm_gain, 1, pairs, 1, temporal)

    frames = (z + jnp.array(REL, jnp.int32)) % planes

    with jax.named_scope("temporal"):
        order = frame_order.astype(jnp.float32)[frames]
        distance = jnp.abs(order[:, None] - order[None, :])
        pair_global = (z * pairs + jnp.arange(pairs, dtype=jnp.int32)).astype(jnp.float32)
        slope = jnp.exp2(-(pair_global + 1.0) * 2.0 / HP)
        tmask = lax.dynamic_index_in_dim(temporal_mask, seq_index, 1, keepdims=False)
        tmask = tmask[:, frames][:, :, frames]
        bias_t = jnp.where(tmask > 0, -slope[:, None, None] * distance[None] * LOG2E, OFF)
        bias_t = jnp.repeat(bias_t, tokens, axis=2)[:, :, None, :]
        temporal_out = temporal_attention(temporal, bias_t)
        temporal_far = along_z(temporal_out[1:], 2)

    with jax.named_scope("spatial"):
        smask = lax.dynamic_index_in_dim(
            spatial_mask, jnp.minimum(x, pairs - 1), 0, keepdims=False
        )
        slot_frame = (z + jnp.array(REL, jnp.int32)[y]) % planes
        smask = lax.dynamic_index_in_dim(smask, slot_frame, 0, keepdims=False)
        smask = smask.reshape(chips, 2, chips, 2)
        smask = lax.dynamic_index_in_dim(smask, core, 1, keepdims=False)
        own_keys = lax.dynamic_index_in_dim(smask, core, 2, keepdims=False)
        other_keys = lax.dynamic_index_in_dim(smask, 1 - core, 2, keepdims=False)
        smask = jnp.concatenate([own_keys, other_keys], axis=1).T
        bias_s = jnp.where(smask > 0, 0.0, OFF).astype(jnp.float32)
        bias_s = jnp.pad(bias_s, ((0, 0), (0, HD - chips)))
        mine = lax.all_to_all(
            spatial.reshape(chips, tokens, 3 * HD), ("y", "x"), 0, 0, tiled=True
        )
        mine, temporal_out, temporal_far, bias_s, out_weight = lax.optimization_barrier(
            (mine, temporal_out, temporal_far, bias_s, out_weight)
        )
        other = swap_cores(mine)
        partial = spatial_attention(mine, mine, bias_s)
        spatial_out = spatial_attention(mine, other, bias_s, partial)
        spatial_out = lax.all_to_all(spatial_out, ("y", "x"), 0, 0, tiled=True)
        spatial_out = spatial_out.reshape(4, 4, tokens, HD)
        spatial_far = along_z(spatial_out[1:, :pairs], 2)

    with jax.named_scope("project"):
        own_heads, far_heads = [spatial_out, temporal_out], [spatial_far, temporal_far]
        sent = project(
            "project_sent_own_group", (1, -1), (0,), own_heads, out_weight, jnp.float32, WIDE
        )
        low, high = project(
            "project_sent", (1, -1), (1,), far_heads, out_weight, jnp.bfloat16, NARROW, sent
        )
        low = along_z(low, 1)
        high = along_z(high, -1)
        kept = project(
            "project_kept", (0,), (0, 1), own_heads + far_heads, out_weight, jnp.bfloat16, NARROW
        )
        return combine(kept, low, high, gate_mod)[None]


def solution(mesh):
    split = Mesh(mesh.devices.reshape(4, 4, 2, 4), ("y", "x", "core", "frm"))
    seq = ("y", "x", "core")
    placed = (
        P("frm", seq, None),
        P(),
        P(),
        P(),
        P(None, "frm", None, None),
        P("frm", None, None),
        P("frm", None, None, seq),
        P("frm", None, None, None),
        P("frm", None, None, None),
        P(),
    )
    return jax.shard_map(
        local, mesh=split, in_specs=placed, out_specs=P("frm", seq, None), check_vma=False
    )
```

```python
import math

import jax
import jax.numpy as jnp
from jax import lax
from jax.experimental import pallas as pl
from jax.experimental.pallas import tpu as pltpu
from jax.sharding import Mesh, PartitionSpec as P

HP = 12
BLK = 128
HD = 128
EPS = 1e-06
LOG2E = 1.4426950408889634
OFF = -1e30
REL = (0, 2, 1, -1)
VMEM = 30 * 1024 * 1024
WIDE, NARROW = 40 * 1024 * 1024, 16 * 1024 * 1024


def params(limit=VMEM):
    return pltpu.CompilerParams(vmem_limit_bytes=limit)


def whole():
    return pl.BlockSpec(memory_space=pltpu.VMEM)


def cost(flops, size, trans=0):
    return pl.CostEstimate(flops=int(flops), bytes_accessed=int(size), transcendentals=int(trans))


def modulate_kernel(hidden_ref, shift_ref, scale_ref, low_ref, high_ref):
    rows = low_ref.shape[0]
    for at, out_ref in ((0, low_ref), (rows, high_ref)):
        values = hidden_ref[at : at + rows].astype(jnp.float32)
        centred = values - jnp.mean(values, axis=-1, keepdims=True)
        spread = jnp.mean(centred * centred, axis=-1, keepdims=True)
        out_ref[...] = (
            centred * lax.rsqrt(spread + EPS) * (1.0 + scale_ref[...]) + shift_ref[...]
        ).astype(jnp.bfloat16)


def modulate(hidden, shift_mod, scale_mod):
    rows, width = hidden.shape
    return pl.pallas_call(
        modulate_kernel,
        in_specs=[whole()] * 3,
        out_specs=[whole()] * 2,
        out_shape=[jax.ShapeDtypeStruct((rows // 2, width), jnp.bfloat16)] * 2,
        compiler_params=params(),
        cost_estimate=cost(10 * rows * width, 4 * rows * width),
        name="modulate",
    )(hidden, shift_mod[None], scale_mod[None])


def heads_kernel(parts, aliased, *refs):
    x_refs = refs[:parts]
    w_ref, gain_ref = refs[parts : parts + 2]
    out_ref, rows_ref = refs[parts + 2 + aliased :]
    pair = pl.program_id(0)
    frames, _, tokens, _ = out_ref.shape

    @pl.when(pair == 0)
    def _():
        at = 0
        for ref in x_refs:
            rows_ref[at : at + ref.shape[0], :] = ref[...]
            at += ref.shape[0]

    weight = jnp.concatenate([w_ref[0, j] for j in range(3)], axis=1)
    projected = jnp.dot(rows_ref[...], weight, preferred_element_type=jnp.float32)
    gains = gain_ref[pair]
    for j in range(3):
        v = projected[:, j * HD : (j + 1) * HD]
        if j < 2:
            square_mean = jnp.mean(v * v, axis=-1, keepdims=True)
            v = v * lax.rsqrt(square_mean + EPS) * gains[j : j + 1]
        out_ref[:, 0, :, j * HD : (j + 1) * HD] = v.astype(jnp.bfloat16).reshape(
            frames, tokens, HD
        )


def heads_both_kernel(parts, aliased, *refs):
    x_refs = refs[:parts]
    w_ref, gain_ref = refs[parts : parts + 2]
    spatial_ref, temporal_ref, rows_ref = refs[parts + 2 + aliased :]
    pair = pl.program_id(0)
    frames, _, tokens, _ = spatial_ref.shape

    @pl.when(pair == 0)
    def _():
        at = 0
        for ref in x_refs:
            rows_ref[at : at + ref.shape[0], :] = ref[...]
            at += ref.shape[0]

    weight = jnp.concatenate([w_ref[0, j] for j in range(6)], axis=1)
    projected = jnp.dot(rows_ref[...], weight, preferred_element_type=jnp.float32)
    for kind, out_ref in enumerate((spatial_ref, temporal_ref)):
        gains = gain_ref[kind, pair]
        for j in range(3):
            at = (kind * 3 + j) * HD
            v = projected[:, at : at + HD]
            if j < 2:
                square_mean = jnp.mean(v * v, axis=-1, keepdims=True)
                v = v * lax.rsqrt(square_mean + EPS) * gains[j : j + 1]
            out_ref[:, 0, :, j * HD : (j + 1) * HD] = v.astype(jnp.bfloat16).reshape(
                frames, tokens, HD
            )


def heads_both(pieces, weight, norm_gain, first, buffers=None):
    parts = len(pieces)
    width = pieces[0].shape[1]
    rows = sum(piece.shape[0] for piece in pieces)
    pairs = weight.shape[0]
    frames = rows // BLK
    triple = 3 * HD
    in_specs = [pl.BlockSpec(piece.shape, lambda n: (0, 0)) for piece in pieces]
    in_specs += [
        pl.BlockSpec((1, 6, width, HD), lambda n: (n, 0, 0, 0)),
        pl.BlockSpec((2, pairs, 2, HD), lambda n: (0, 0, 0, 0)),
    ]
    args = list(pieces) + [weight, norm_gain]
    aliases = {}
    if buffers is not None:
        in_specs += [pl.BlockSpec(memory_space=pl.ANY)] * 2
        aliases = {len(args): 0, len(args) + 1: 1}
        args += list(buffers)
    out_spec = pl.BlockSpec((frames, 1, BLK, triple), lambda n: (first // frames, n, 0, 0))
    return pl.pallas_call(
        lambda *refs: heads_both_kernel(parts, 2 * (buffers is not None), *refs),
        grid=(pairs,),
        in_specs=in_specs,
        out_specs=[out_spec, out_spec],
        out_shape=[
            jax.ShapeDtypeStruct((4, slots, BLK, triple), jnp.bfloat16) for slots in (4, pairs)
        ],
        scratch_shapes=[pltpu.VMEM((rows, width), jnp.bfloat16)],
        input_output_aliases=aliases,
        compiler_params=params(WIDE),
        cost_estimate=cost(4 * rows * width * pairs * triple, width * pairs * triple * 4),
        name="qkv_both",
    )(*args)


def heads(pieces, weight, norm_gain, kind, slots, first, buffer=None):
    parts = len(pieces)
    width = pieces[0].shape[1]
    rows = sum(piece.shape[0] for piece in pieces)
    pairs = weight.shape[0]
    block = kind if weight.shape[1] > 3 else 0
    frames = rows // BLK
    triple = 3 * HD
    aliased = buffer is not None
    in_specs = [pl.BlockSpec(piece.shape, lambda n: (0, 0)) for piece in pieces]
    in_specs += [
        pl.BlockSpec((1, 3, width, HD), lambda n: (n, block, 0, 0)),
        pl.BlockSpec((pairs, 2, HD), lambda n: (0, 0, 0)),
    ]
    args = list(pieces) + [weight, norm_gain[kind]]
    aliases = {}
    if aliased:
        in_specs.append(pl.BlockSpec(memory_space=pl.ANY))
        aliases = {len(args): 0}
        args.append(buffer)

    def body(*refs):
        heads_kernel(parts, int(aliased), *refs)

    return pl.pallas_call(
        body,
        grid=(pairs,),
        in_specs=in_specs,
        out_specs=pl.BlockSpec((frames, 1, BLK, triple), lambda n: (first // frames, n, 0, 0)),
        out_shape=jax.ShapeDtypeStruct((4, slots, BLK, triple), jnp.bfloat16),
        scratch_shapes=[pltpu.VMEM((rows, width), jnp.bfloat16)],
        input_output_aliases=aliases,
        compiler_params=params(),
        cost_estimate=cost(2 * rows * width * pairs * triple, width * pairs * triple * 2),
        name="qkv_spatial" if kind == 0 else "qkv_temporal",
    )(*args)


def spatial_kernel(side, own_ref, keys_ref, bias_ref, *refs):
    blocks = own_ref.shape[0]
    rows = blocks * BLK
    shape = (blocks, BLK, HD)
    one_hot = lax.broadcasted_iota(jnp.int32, shape, 2) == lax.broadcasted_iota(jnp.int32, shape, 0)
    one_hot = jnp.where(one_hot, 1.0, 0.0).astype(jnp.bfloat16)
    queries = jnp.concatenate([own_ref[:, :, 0:HD], one_hot], axis=2).reshape(rows, 2 * HD)
    per_chunk = 4
    chunk = per_chunk * BLK
    ones = jnp.ones((chunk, HD), jnp.bfloat16)
    out_ref = refs[-1]
    summed = jnp.zeros((rows, 2 * HD), jnp.float32) if side == 0 else refs[0][...]
    for ref in (keys_ref,):
        for at in range(0, blocks, per_chunk):
            row = side * blocks + at
            bias = jnp.concatenate(
                [
                    jnp.broadcast_to(bias_ref[row + i : row + i + 1, :], (BLK, HD))
                    for i in range(per_chunk)
                ],
                axis=0,
            ).astype(jnp.bfloat16)
            keys = ref[at : at + per_chunk, :, HD : 2 * HD].reshape(chunk, HD)
            values = ref[at : at + per_chunk, :, 2 * HD :].reshape(chunk, HD)
            scores = lax.dot_general(
                queries, jnp.concatenate([keys, bias], axis=1), (((1,), (1,)), ((), ())),
                preferred_element_type=jnp.float32,
            )
            summed = summed + jnp.dot(
                jnp.exp2(scores).astype(jnp.bfloat16), jnp.concatenate([values, ones], axis=1),
                preferred_element_type=jnp.float32,
            )
    if side == 0:
        out_ref[...] = summed
        return
    out_ref[...] = (summed[:, :HD] / summed[:, HD:]).astype(jnp.bfloat16).reshape(shape)


def spatial_attention(own, keys, bias, partial=None):
    blocks, tokens, triple = own.shape
    rows = blocks * tokens
    side = 0 if partial is None else 1
    args = [own, keys, bias] + ([] if partial is None else [partial])
    out = ((rows, 2 * HD), jnp.float32) if side == 0 else ((blocks, tokens, HD), jnp.bfloat16)
    return pl.pallas_call(
        lambda *refs: spatial_kernel(side, *refs),
        in_specs=[whole()] * len(args),
        out_specs=whole(),
        out_shape=jax.ShapeDtypeStruct(*out),
        compiler_params=params(),
        cost_estimate=cost(8 * rows * rows * HD, 4 * rows * triple, rows * rows),
        name=("spatial_attention_own", "spatial_attention_other")[side],
    )(*args)


def temporal_kernel(qkv_ref, bias_ref, out_ref):
    frames, _, tokens, _ = qkv_ref.shape
    rows = frames * tokens
    queries = qkv_ref[:, 0, :, 0:HD].reshape(rows, HD)
    keys = qkv_ref[:, 0, :, HD : 2 * HD].reshape(rows, HD)
    values = qkv_ref[:, 0, :, 2 * HD :].reshape(rows, HD)
    values = jnp.concatenate([values, jnp.ones((rows, HD), jnp.bfloat16)], axis=1)
    scores = lax.dot_general(
        queries, keys, (((1,), (1,)), ((), ())), preferred_element_type=jnp.float32
    )
    scores = scores.reshape(frames, tokens, rows) + bias_ref[0]
    weights = jnp.exp2(scores).astype(jnp.bfloat16).reshape(rows, rows)
    summed = jnp.dot(weights, values, preferred_element_type=jnp.float32)
    result = (summed[:, :HD] / summed[:, HD:]).astype(jnp.bfloat16)
    out_ref[:, 0] = result.reshape(frames, tokens, HD)


def temporal_attention(qkv, bias):
    frames, pairs, tokens, triple = qkv.shape
    rows = frames * tokens
    return pl.pallas_call(
        temporal_kernel,
        grid=(pairs,),
        in_specs=[
            pl.BlockSpec((frames, 1, tokens, triple), lambda h: (0, h, 0, 0)),
            pl.BlockSpec((1, frames, 1, rows), lambda h: (h, 0, 0, 0)),
        ],
        out_specs=pl.BlockSpec((frames, 1, tokens, HD), lambda h: (0, h, 0, 0)),
        out_shape=jax.ShapeDtypeStruct((frames, pairs, tokens, HD), jnp.bfloat16),
        compiler_params=params(),
        cost_estimate=cost(6 * pairs * rows * rows * HD, 2 * frames * pairs * tokens * triple),
        name="temporal_attention",
    )(qkv, bias)


OWN_SLOT = {0: 0, 1: 2, -1: 3}
FAR_SLOT = {0: 0, 1: 2, -1: 1}


def project_kernel(targets, groups, used, has_partial, *refs):
    heads_count = len(used) * len(groups)
    head_refs, w_ref = refs[:heads_count], refs[heads_count]
    rest, rows_ref = refs[heads_count + 1 : -1], refs[-1]
    step, steps = pl.program_id(0), pl.num_programs(0)
    shards, _, pairs, kinds, columns, _ = w_ref.shape
    depth = pairs * kinds * HD

    @pl.when(step == 0)
    def _():
        for number, target in enumerate(targets):
            for at_group, group in enumerate(groups):
                slot = (OWN_SLOT, FAR_SLOT)[group][target]
                for kind in range(kinds):
                    ref = head_refs[len(used) * at_group + kind]
                    for pair in range(pairs):
                        at = at_group * depth + (pair * kinds + kind) * HD
                        rows_ref[number, :, at : at + HD] = ref[slot, pair]

    weight = jnp.concatenate(
        [
            w_ref[:, at_group, pair, kind].reshape(shards * columns, HD)
            for at_group in range(len(groups))
            for pair in range(pairs)
            for kind in range(kinds)
        ],
        axis=1,
    )
    rows = rows_ref[step * len(targets) // steps]
    product = lax.dot_general(
        rows, weight, (((1,), (1,)), ((), ())), preferred_element_type=jnp.float32
    )
    if has_partial:
        product = product + rest[0][...]
        rest = rest[1:]
    product = product.astype(rest[0].dtype)
    if len(rest) == 1:
        rest[0][...] = product
        return
    low_ref, high_ref = rest

    @pl.when(step < steps // 2)
    def _():
        low_ref[...] = product

    @pl.when(step >= steps // 2)
    def _():
        high_ref[...] = product


def project(
    name, targets, groups, used, head_arrays, weight, dtype, limit, partial=None, split=False
):
    shards, _, pairs, _, shard, _ = weight.shape
    kinds = len(used)
    per_step = 8
    steps, width = shards // per_step, per_step * shard
    depth = len(groups) * kinds * pairs * HD
    first = groups[0] // len(groups)
    first_kind = used[0] // kinds
    column = pl.BlockSpec((BLK, width), lambda n: (0, n))
    partials = [] if partial is None else [partial]
    if not split:
        out_specs = column
        out_shape = jax.ShapeDtypeStruct((BLK, steps * width), dtype)
    else:
        out_specs = [
            pl.BlockSpec((BLK, width), lambda n: (0, jnp.minimum(n, steps // 2 - 1))),
            pl.BlockSpec((BLK, width), lambda n: (0, jnp.maximum(n - steps // 2, 0))),
        ]
        out_shape = [jax.ShapeDtypeStruct((BLK, steps // 2 * width), dtype)] * 2
    return pl.pallas_call(
        lambda *refs: project_kernel(targets, groups, used, partial is not None, *refs),
        grid=(steps,),
        in_specs=[pl.BlockSpec(array.shape, lambda n: (0, 0, 0, 0)) for array in head_arrays]
        + [
            pl.BlockSpec(
                (per_step, len(groups), pairs, kinds, shard, HD),
                lambda n: (n, first, 0, first_kind, 0, 0),
            )
        ]
        + [column] * len(partials),
        out_specs=out_specs,
        out_shape=out_shape,
        scratch_shapes=[pltpu.VMEM((len(targets), BLK, depth), jnp.bfloat16)],
        compiler_params=params(limit),
        cost_estimate=cost(2 * BLK * steps * width * depth, 2 * steps * width * depth),
        name=name,
    )(*head_arrays, weight, *partials)


def combine_kernel(own_ref, low_ref, high_ref, gate_ref, out_ref):
    step, steps = pl.program_id(0), pl.num_programs(0)

    def write(ref):
        branch = own_ref[...].astype(jnp.float32) + ref[...].astype(jnp.float32)
        out_ref[...] = (gate_ref[...] * branch).astype(jnp.bfloat16)

    @pl.when(step < steps // 2)
    def _():
        write(low_ref)

    @pl.when(step >= steps // 2)
    def _():
        write(high_ref)


def combine(own, low, high, gate):
    rows, width = own.shape
    steps = 2
    each = width // steps
    column = pl.BlockSpec((rows, each), lambda n: (0, n))
    return pl.pallas_call(
        combine_kernel,
        grid=(steps,),
        in_specs=[
            column,
            pl.BlockSpec((rows, each), lambda n: (0, jnp.minimum(n, steps // 2 - 1))),
            pl.BlockSpec((rows, each), lambda n: (0, jnp.maximum(n - steps // 2, 0))),
            pl.BlockSpec((1, each), lambda n: (0, n)),
        ],
        out_specs=column,
        out_shape=jax.ShapeDtypeStruct((rows, width), jnp.bfloat16),
        compiler_params=params(),
        cost_estimate=cost(3 * rows * width, 10 * rows * width),
        name="combine",
    )(own, low, high, gate[None])


def local(
    hidden_in,
    shift_mod,
    scale_mod,
    gate_mod,
    w_qkv,
    norm_gain,
    w_out,
    spatial_mask,
    temporal_mask,
    frame_order,
):
    tokens = hidden_in.shape[1]
    pairs = w_qkv.shape[1]
    y, x, core, z = (lax.axis_index(name) for name in ("y", "x", "core", "frm"))
    chips = lax.axis_size("y") * lax.axis_size("x")
    planes = lax.axis_size("frm")
    chip = y * lax.axis_size("x") + x
    seq_index = chip * 2 + core

    def along_z(value, shift):
        return lax.ppermute(value, "frm", [(i, (i + shift) % planes) for i in range(planes)])

    def swap_cores(value):
        return lax.ppermute(value, "core", [(0, 1), (1, 0)])

    with jax.named_scope("modulate"):
        own = modulate(hidden_in[0], shift_mod, scale_mod)

    with jax.named_scope("gather_w_out"):
        turned = jnp.transpose(w_out, (0, 1, 3, 2))
        (low, high), turned_far = lax.optimization_barrier((own, along_z(turned, 2)))
        out_weight = jnp.stack([turned, turned_far])
        out_weight = lax.all_gather(out_weight, ("y", "x", "core"), axis=0, tiled=False)

    with jax.named_scope("qkv"):
        weight = jnp.transpose(w_qkv, (1, 2, 0, 3))
        factor = jnp.array([LOG2E / math.sqrt(HD), 1.0], jnp.float32)
        norm_gain = jnp.transpose(norm_gain.reshape(pairs, 2, 2, HD), (1, 0, 2, 3))
        norm_gain = norm_gain * factor[None, None, :, None]
        before_low, after_high = along_z(low, 1), along_z(high, -1)
        before_high, after_low = along_z(high, 1), along_z(low, -1)
        spatial, temporal = heads_both([low, high], weight, norm_gain, 0)
        before_low, after_high, spatial, temporal = lax.optimization_barrier(
            (before_low, after_high, spatial, temporal)
        )
        far = [along_z(before_low, 1), along_z(after_high, -1)]
        spatial, temporal = heads_both(
            [after_low, after_high, before_low, before_high],
            weight,
            norm_gain,
            2,
            (spatial, temporal),
        )
        far, spatial, temporal = lax.optimization_barrier((far, spatial, temporal))
        spatial = heads(far, weight, norm_gain, 0, 4, 1, spatial)
        spatial, far = lax.optimization_barrier((spatial, far))
        temporal = heads(far, weight, norm_gain, 1, pairs, 1, temporal)

    frames = (z + jnp.array(REL, jnp.int32)) % planes

    with jax.named_scope("temporal"):
        order = frame_order.astype(jnp.float32)[frames]
        distance = jnp.abs(order[:, None] - order[None, :])
        pair_global = (z * pairs + jnp.arange(pairs, dtype=jnp.int32)).astype(jnp.float32)
        slope = jnp.exp2(-(pair_global + 1.0) * 2.0 / HP)
        tmask = lax.dynamic_index_in_dim(temporal_mask, seq_index, 1, keepdims=False)
        tmask = tmask[:, frames][:, :, frames]
        bias_t = jnp.where(tmask > 0, -slope[:, None, None] * distance[None] * LOG2E, OFF)
        bias_t = jnp.repeat(bias_t, tokens, axis=2)[:, :, None, :]
        temporal_out = temporal_attention(temporal, bias_t)
        temporal_far = along_z(temporal_out[1:], 2)

    with jax.named_scope("spatial"):
        smask = lax.dynamic_index_in_dim(
            spatial_mask, jnp.minimum(x, pairs - 1), 0, keepdims=False
        )
        slot_frame = (z + jnp.array(REL, jnp.int32)[y]) % planes
        smask = lax.dynamic_index_in_dim(smask, slot_frame, 0, keepdims=False)
        smask = smask.reshape(chips, 2, chips, 2)
        smask = lax.dynamic_index_in_dim(smask, core, 1, keepdims=False)
        own_keys = lax.dynamic_index_in_dim(smask, core, 2, keepdims=False)
        other_keys = lax.dynamic_index_in_dim(smask, 1 - core, 2, keepdims=False)
        smask = jnp.concatenate([own_keys, other_keys], axis=1).T
        bias_s = jnp.where(smask > 0, 0.0, OFF).astype(jnp.float32)
        bias_s = jnp.pad(bias_s, ((0, 0), (0, HD - chips)))
        mine = lax.all_to_all(
            spatial.reshape(chips, tokens, 3 * HD), ("y", "x"), 0, 0, tiled=True
        )
        mine, temporal_out, temporal_far, bias_s, out_weight = lax.optimization_barrier(
            (mine, temporal_out, temporal_far, bias_s, out_weight)
        )
        sent = project(
            "project_sent_temporal",
            (1, -1), (0, 1), (1,), [temporal_out, temporal_far], out_weight, jnp.float32, WIDE,
        )
        other = swap_cores(mine)
        partial = spatial_attention(mine, mine, bias_s)
        spatial_out = spatial_attention(mine, other, bias_s, partial)
        spatial_out = lax.all_to_all(spatial_out, ("y", "x"), 0, 0, tiled=True)
        spatial_out = spatial_out.reshape(4, 4, tokens, HD)
        spatial_far = along_z(spatial_out[1:, :pairs], 2)

    with jax.named_scope("project"):
        sent = project(
            "project_sent_own_spatial",
            (1, -1), (0,), (0,), [spatial_out], out_weight, jnp.float32, WIDE, sent,
        )
        low, high = project(
            "project_sent",
            (1, -1), (1,), (0,), [spatial_far], out_weight, jnp.bfloat16, NARROW, sent, True,
        )
        low = along_z(low, 1)
        high = along_z(high, -1)
        head_arrays = [spatial_out, temporal_out, spatial_far, temporal_far]
        kept = project(
            "project_kept", (0,), (0, 1), (0, 1), head_arrays, out_weight, jnp.bfloat16, NARROW
        )
        return combine(kept, low, high, gate_mod)[None]


def solution(mesh):
    split = Mesh(mesh.devices.reshape(4, 4, 2, 4), ("y", "x", "core", "frm"))
    seq = ("y", "x", "core")
    placed = (
        P("frm", seq, None),
        P(),
        P(),
        P(),
        P(None, "frm", None, None),
        P("frm", None, None),
        P("frm", None, None, seq),
        P("frm", None, None, None),
        P("frm", None, None, None),
        P(),
    )
    return jax.shard_map(
        local, mesh=split, in_specs=placed, out_specs=P("frm", seq, None), check_vma=False
    )
```

```python
import math

import jax
import jax.numpy as jnp
from jax import lax
from jax.experimental import pallas as pl
from jax.experimental.pallas import tpu as pltpu
from jax.sharding import Mesh, PartitionSpec as P

HP = 12
BLK = 128
HD = 128
EPS = 1e-06
LOG2E = 1.4426950408889634
OFF = -1e30
REL = (0, 2, 1, -1)
VMEM = 30 * 1024 * 1024
WIDE, NARROW = 40 * 1024 * 1024, 16 * 1024 * 1024


def params(limit=VMEM):
    return pltpu.CompilerParams(vmem_limit_bytes=limit)


def whole():
    return pl.BlockSpec(memory_space=pltpu.VMEM)


def cost(flops, size, trans=0):
    return pl.CostEstimate(flops=int(flops), bytes_accessed=int(size), transcendentals=int(trans))


def modulate_kernel(hidden_ref, shift_ref, scale_ref, low_ref, high_ref):
    rows = low_ref.shape[0]
    for at, out_ref in ((0, low_ref), (rows, high_ref)):
        values = hidden_ref[at : at + rows].astype(jnp.float32)
        centred = values - jnp.mean(values, axis=-1, keepdims=True)
        spread = jnp.mean(centred * centred, axis=-1, keepdims=True)
        out_ref[...] = (
            centred * lax.rsqrt(spread + EPS) * (1.0 + scale_ref[...]) + shift_ref[...]
        ).astype(jnp.bfloat16)


def modulate(hidden, shift_mod, scale_mod):
    rows, width = hidden.shape
    return pl.pallas_call(
        modulate_kernel,
        in_specs=[whole()] * 3,
        out_specs=[whole()] * 2,
        out_shape=[jax.ShapeDtypeStruct((rows // 2, width), jnp.bfloat16)] * 2,
        compiler_params=params(),
        cost_estimate=cost(10 * rows * width, 4 * rows * width),
        name="modulate",
    )(hidden, shift_mod[None], scale_mod[None])


def heads_kernel(parts, aliased, *refs):
    x_refs = refs[:parts]
    w_ref, gain_ref = refs[parts : parts + 2]
    out_ref, rows_ref = refs[parts + 2 + aliased :]
    pair = pl.program_id(0)
    frames, _, tokens, _ = out_ref.shape

    @pl.when(pair == 0)
    def _():
        at = 0
        for ref in x_refs:
            rows_ref[at : at + ref.shape[0], :] = ref[...]
            at += ref.shape[0]

    weight = jnp.concatenate([w_ref[0, j] for j in range(3)], axis=1)
    projected = jnp.dot(rows_ref[...], weight, preferred_element_type=jnp.float32)
    gains = gain_ref[pair]
    for j in range(3):
        v = projected[:, j * HD : (j + 1) * HD]
        if j < 2:
            square_mean = jnp.mean(v * v, axis=-1, keepdims=True)
            v = v * lax.rsqrt(square_mean + EPS) * gains[j : j + 1]
        out_ref[:, 0, :, j * HD : (j + 1) * HD] = v.astype(jnp.bfloat16).reshape(
            frames, tokens, HD
        )


def heads_both_kernel(parts, aliased, *refs):
    x_refs = refs[:parts]
    w_ref, gain_ref = refs[parts : parts + 2]
    spatial_ref, temporal_ref, rows_ref = refs[parts + 2 + aliased :]
    pair = pl.program_id(0)
    frames, _, tokens, _ = spatial_ref.shape

    @pl.when(pair == 0)
    def _():
        at = 0
        for ref in x_refs:
            rows_ref[at : at + ref.shape[0], :] = ref[...]
            at += ref.shape[0]

    weight = jnp.concatenate([w_ref[0, j] for j in range(6)], axis=1)
    projected = jnp.dot(rows_ref[...], weight, preferred_element_type=jnp.float32)
    for kind, out_ref in enumerate((spatial_ref, temporal_ref)):
        gains = gain_ref[kind, pair]
        for j in range(3):
            at = (kind * 3 + j) * HD
            v = projected[:, at : at + HD]
            if j < 2:
                square_mean = jnp.mean(v * v, axis=-1, keepdims=True)
                v = v * lax.rsqrt(square_mean + EPS) * gains[j : j + 1]
            out_ref[:, 0, :, j * HD : (j + 1) * HD] = v.astype(jnp.bfloat16).reshape(
                frames, tokens, HD
            )


def heads_both(pieces, weight, norm_gain, first, buffers=None):
    parts = len(pieces)
    width = pieces[0].shape[1]
    rows = sum(piece.shape[0] for piece in pieces)
    pairs = weight.shape[0]
    frames = rows // BLK
    triple = 3 * HD
    in_specs = [pl.BlockSpec(piece.shape, lambda n: (0, 0)) for piece in pieces]
    in_specs += [
        pl.BlockSpec((1, 6, width, HD), lambda n: (n, 0, 0, 0)),
        pl.BlockSpec((2, pairs, 2, HD), lambda n: (0, 0, 0, 0)),
    ]
    args = list(pieces) + [weight, norm_gain]
    aliases = {}
    if buffers is not None:
        in_specs += [pl.BlockSpec(memory_space=pl.ANY)] * 2
        aliases = {len(args): 0, len(args) + 1: 1}
        args += list(buffers)
    out_spec = pl.BlockSpec((frames, 1, BLK, triple), lambda n: (first // frames, n, 0, 0))
    return pl.pallas_call(
        lambda *refs: heads_both_kernel(parts, 2 * (buffers is not None), *refs),
        grid=(pairs,),
        in_specs=in_specs,
        out_specs=[out_spec, out_spec],
        out_shape=[
            jax.ShapeDtypeStruct((4, slots, BLK, triple), jnp.bfloat16) for slots in (4, pairs)
        ],
        scratch_shapes=[pltpu.VMEM((rows, width), jnp.bfloat16)],
        input_output_aliases=aliases,
        compiler_params=params(WIDE),
        cost_estimate=cost(4 * rows * width * pairs * triple, width * pairs * triple * 4),
        name="qkv_both",
    )(*args)


def heads(pieces, weight, norm_gain, kind, slots, first, buffer=None):
    parts = len(pieces)
    width = pieces[0].shape[1]
    rows = sum(piece.shape[0] for piece in pieces)
    pairs = weight.shape[0]
    block = kind if weight.shape[1] > 3 else 0
    frames = rows // BLK
    triple = 3 * HD
    aliased = buffer is not None
    in_specs = [pl.BlockSpec(piece.shape, lambda n: (0, 0)) for piece in pieces]
    in_specs += [
        pl.BlockSpec((1, 3, width, HD), lambda n: (n, block, 0, 0)),
        pl.BlockSpec((pairs, 2, HD), lambda n: (0, 0, 0)),
    ]
    args = list(pieces) + [weight, norm_gain[kind]]
    aliases = {}
    if aliased:
        in_specs.append(pl.BlockSpec(memory_space=pl.ANY))
        aliases = {len(args): 0}
        args.append(buffer)

    def body(*refs):
        heads_kernel(parts, int(aliased), *refs)

    return pl.pallas_call(
        body,
        grid=(pairs,),
        in_specs=in_specs,
        out_specs=pl.BlockSpec((frames, 1, BLK, triple), lambda n: (first // frames, n, 0, 0)),
        out_shape=jax.ShapeDtypeStruct((4, slots, BLK, triple), jnp.bfloat16),
        scratch_shapes=[pltpu.VMEM((rows, width), jnp.bfloat16)],
        input_output_aliases=aliases,
        compiler_params=params(),
        cost_estimate=cost(2 * rows * width * pairs * triple, width * pairs * triple * 2),
        name="qkv_spatial" if kind == 0 else "qkv_temporal",
    )(*args)


def spatial_kernel(side, own_ref, keys_ref, bias_ref, *refs):
    blocks = own_ref.shape[0]
    rows = blocks * BLK
    shape = (blocks, BLK, HD)
    one_hot = lax.broadcasted_iota(jnp.int32, shape, 2) == lax.broadcasted_iota(jnp.int32, shape, 0)
    one_hot = jnp.where(one_hot, 1.0, 0.0).astype(jnp.bfloat16)
    queries = jnp.concatenate([own_ref[:, :, 0:HD], one_hot], axis=2).reshape(rows, 2 * HD)
    per_chunk = 4
    chunk = per_chunk * BLK
    ones = jnp.ones((chunk, HD), jnp.bfloat16)
    out_ref = refs[-1]
    summed = jnp.zeros((rows, 2 * HD), jnp.float32) if side == 0 else refs[0][...]
    for ref in (keys_ref,):
        for at in range(0, blocks, per_chunk):
            row = side * blocks + at
            bias = jnp.concatenate(
                [
                    jnp.broadcast_to(bias_ref[row + i : row + i + 1, :], (BLK, HD))
                    for i in range(per_chunk)
                ],
                axis=0,
            ).astype(jnp.bfloat16)
            keys = ref[at : at + per_chunk, :, HD : 2 * HD].reshape(chunk, HD)
            values = ref[at : at + per_chunk, :, 2 * HD :].reshape(chunk, HD)
            scores = lax.dot_general(
                queries, jnp.concatenate([keys, bias], axis=1), (((1,), (1,)), ((), ())),
                preferred_element_type=jnp.float32,
            )
            summed = summed + jnp.dot(
                jnp.exp2(scores).astype(jnp.bfloat16), jnp.concatenate([values, ones], axis=1),
                preferred_element_type=jnp.float32,
            )
    if side == 0:
        out_ref[...] = summed
        return
    out_ref[...] = (summed[:, :HD] / summed[:, HD:]).astype(jnp.bfloat16).reshape(shape)


def spatial_attention(own, keys, bias, partial=None):
    blocks, tokens, triple = own.shape
    rows = blocks * tokens
    side = 0 if partial is None else 1
    args = [own, keys, bias] + ([] if partial is None else [partial])
    out = ((rows, 2 * HD), jnp.float32) if side == 0 else ((blocks, tokens, HD), jnp.bfloat16)
    return pl.pallas_call(
        lambda *refs: spatial_kernel(side, *refs),
        in_specs=[whole()] * len(args),
        out_specs=whole(),
        out_shape=jax.ShapeDtypeStruct(*out),
        compiler_params=params(),
        cost_estimate=cost(8 * rows * rows * HD, 4 * rows * triple, rows * rows),
        name=("spatial_attention_own", "spatial_attention_other")[side],
    )(*args)


def temporal_kernel(qkv_ref, bias_ref, out_ref):
    frames, _, tokens, _ = qkv_ref.shape
    rows = frames * tokens
    queries = qkv_ref[:, 0, :, 0:HD].reshape(rows, HD)
    keys = qkv_ref[:, 0, :, HD : 2 * HD].reshape(rows, HD)
    values = qkv_ref[:, 0, :, 2 * HD :].reshape(rows, HD)
    values = jnp.concatenate([values, jnp.ones((rows, HD), jnp.bfloat16)], axis=1)
    scores = lax.dot_general(
        queries, keys, (((1,), (1,)), ((), ())), preferred_element_type=jnp.float32
    )
    scores = scores.reshape(frames, tokens, rows) + bias_ref[0]
    weights = jnp.exp2(scores).astype(jnp.bfloat16).reshape(rows, rows)
    summed = jnp.dot(weights, values, preferred_element_type=jnp.float32)
    result = (summed[:, :HD] / summed[:, HD:]).astype(jnp.bfloat16)
    out_ref[:, 0] = result.reshape(frames, tokens, HD)


def temporal_attention(qkv, bias):
    frames, pairs, tokens, triple = qkv.shape
    rows = frames * tokens
    return pl.pallas_call(
        temporal_kernel,
        grid=(pairs,),
        in_specs=[
            pl.BlockSpec((frames, 1, tokens, triple), lambda h: (0, h, 0, 0)),
            pl.BlockSpec((1, frames, 1, rows), lambda h: (h, 0, 0, 0)),
        ],
        out_specs=pl.BlockSpec((frames, 1, tokens, HD), lambda h: (0, h, 0, 0)),
        out_shape=jax.ShapeDtypeStruct((frames, pairs, tokens, HD), jnp.bfloat16),
        compiler_params=params(),
        cost_estimate=cost(6 * pairs * rows * rows * HD, 2 * frames * pairs * tokens * triple),
        name="temporal_attention",
    )(qkv, bias)


OWN_SLOT = {0: 0, 1: 2, -1: 3}
FAR_SLOT = {0: 0, 1: 2, -1: 1}


def project_kernel(targets, groups, *refs):
    heads_count = 2 * len(groups)
    head_refs, w_ref = refs[:heads_count], refs[heads_count]
    rest, rows_ref = refs[heads_count + 1 : -1], refs[-1]
    step, steps = pl.program_id(0), pl.num_programs(0)
    shards, _, pairs, kinds, columns, _ = w_ref.shape
    depth = pairs * kinds * HD

    @pl.when(step == 0)
    def _():
        for number, target in enumerate(targets):
            for at_group, group in enumerate(groups):
                slot = (OWN_SLOT, FAR_SLOT)[group][target]
                for kind in range(kinds):
                    ref = head_refs[2 * at_group + kind]
                    for pair in range(pairs):
                        at = at_group * depth + (pair * kinds + kind) * HD
                        rows_ref[number, :, at : at + HD] = ref[slot, pair]

    weight = jnp.concatenate(
        [
            w_ref[:, at_group, pair, kind].reshape(shards * columns, HD)
            for at_group in range(len(groups))
            for pair in range(pairs)
            for kind in range(kinds)
        ],
        axis=1,
    )
    rows = rows_ref[step * len(targets) // steps]
    product = lax.dot_general(
        rows, weight, (((1,), (1,)), ((), ())), preferred_element_type=jnp.float32
    )
    if len(rest) == 1:
        rest[0][...] = product.astype(rest[0].dtype)
        return
    partial_ref, low_ref, high_ref = rest
    product = (product + partial_ref[...]).astype(jnp.bfloat16)

    @pl.when(step < steps // 2)
    def _():
        low_ref[...] = product

    @pl.when(step >= steps // 2)
    def _():
        high_ref[...] = product


def project(name, targets, groups, head_arrays, weight, dtype, limit, partial=None):
    shards, _, pairs, kinds, shard, _ = weight.shape
    per_step = 8 if partial is None else 16
    steps, width = shards // per_step, per_step * shard
    depth = len(groups) * kinds * pairs * HD
    first = groups[0] // len(groups)
    column = pl.BlockSpec((BLK, width), lambda n: (0, n))
    partials = [] if partial is None else [partial]
    if partial is None:
        out_specs = column
        out_shape = jax.ShapeDtypeStruct((BLK, steps * width), dtype)
    else:
        out_specs = [
            pl.BlockSpec((BLK, width), lambda n: (0, jnp.minimum(n, steps // 2 - 1))),
            pl.BlockSpec((BLK, width), lambda n: (0, jnp.maximum(n - steps // 2, 0))),
        ]
        out_shape = [jax.ShapeDtypeStruct((BLK, steps // 2 * width), dtype)] * 2
    return pl.pallas_call(
        lambda *refs: project_kernel(targets, groups, *refs),
        grid=(steps,),
        in_specs=[pl.BlockSpec(array.shape, lambda n: (0, 0, 0, 0)) for array in head_arrays]
        + [
            pl.BlockSpec(
                (per_step, len(groups), pairs, kinds, shard, HD),
                lambda n: (n, first, 0, 0, 0, 0),
            )
        ]
        + [column] * len(partials),
        out_specs=out_specs,
        out_shape=out_shape,
        scratch_shapes=[pltpu.VMEM((len(targets), BLK, depth), jnp.bfloat16)],
        compiler_params=params(limit),
        cost_estimate=cost(2 * BLK * steps * width * depth, 2 * steps * width * depth),
        name=name,
    )(*head_arrays, weight, *partials)


def combine_kernel(own_ref, low_ref, high_ref, gate_ref, out_ref):
    step, steps = pl.program_id(0), pl.num_programs(0)

    def write(ref):
        branch = own_ref[...].astype(jnp.float32) + ref[...].astype(jnp.float32)
        out_ref[...] = (gate_ref[...] * branch).astype(jnp.bfloat16)

    @pl.when(step < steps // 2)
    def _():
        write(low_ref)

    @pl.when(step >= steps // 2)
    def _():
        write(high_ref)


def combine(own, low, high, gate):
    rows, width = own.shape
    steps = 2
    each = width // steps
    column = pl.BlockSpec((rows, each), lambda n: (0, n))
    return pl.pallas_call(
        combine_kernel,
        grid=(steps,),
        in_specs=[
            column,
            pl.BlockSpec((rows, each), lambda n: (0, jnp.minimum(n, steps // 2 - 1))),
            pl.BlockSpec((rows, each), lambda n: (0, jnp.maximum(n - steps // 2, 0))),
            pl.BlockSpec((1, each), lambda n: (0, n)),
        ],
        out_specs=column,
        out_shape=jax.ShapeDtypeStruct((rows, width), jnp.bfloat16),
        compiler_params=params(),
        cost_estimate=cost(3 * rows * width, 10 * rows * width),
        name="combine",
    )(own, low, high, gate[None])


def local(
    hidden_in,
    shift_mod,
    scale_mod,
    gate_mod,
    w_qkv,
    norm_gain,
    w_out,
    spatial_mask,
    temporal_mask,
    frame_order,
):
    tokens = hidden_in.shape[1]
    pairs = w_qkv.shape[1]
    y, x, core, z = (lax.axis_index(name) for name in ("y", "x", "core", "frm"))
    chips = lax.axis_size("y") * lax.axis_size("x")
    planes = lax.axis_size("frm")
    chip = y * lax.axis_size("x") + x
    seq_index = chip * 2 + core

    def along_z(value, shift):
        return lax.ppermute(value, "frm", [(i, (i + shift) % planes) for i in range(planes)])

    def swap_cores(value):
        return lax.ppermute(value, "core", [(0, 1), (1, 0)])

    with jax.named_scope("modulate"):
        own = modulate(hidden_in[0], shift_mod, scale_mod)

    with jax.named_scope("gather_w_out"):
        turned = jnp.transpose(w_out, (0, 1, 3, 2))
        (low, high), turned_far = lax.optimization_barrier((own, along_z(turned, 2)))
        out_weight = jnp.stack([turned, turned_far])
        out_weight = lax.all_gather(out_weight, ("y", "x", "core"), axis=0, tiled=False)

    with jax.named_scope("qkv"):
        weight = jnp.transpose(w_qkv, (1, 2, 0, 3))
        factor = jnp.array([LOG2E / math.sqrt(HD), 1.0], jnp.float32)
        norm_gain = jnp.transpose(norm_gain.reshape(pairs, 2, 2, HD), (1, 0, 2, 3))
        norm_gain = norm_gain * factor[None, None, :, None]
        before_low, after_high = along_z(low, 1), along_z(high, -1)
        before_high, after_low = along_z(high, 1), along_z(low, -1)
        spatial, temporal = heads_both([low, high], weight, norm_gain, 0)
        before_low, after_high, spatial, temporal = lax.optimization_barrier(
            (before_low, after_high, spatial, temporal)
        )
        far = [along_z(before_low, 1), along_z(after_high, -1)]
        spatial, temporal = heads_both(
            [after_low, after_high, before_low, before_high],
            weight,
            norm_gain,
            2,
            (spatial, temporal),
        )
        far, spatial, temporal = lax.optimization_barrier((far, spatial, temporal))
        spatial = heads(far, weight, norm_gain, 0, 4, 1, spatial)
        spatial, far = lax.optimization_barrier((spatial, far))
        temporal = heads(far, weight, norm_gain, 1, pairs, 1, temporal)

    frames = (z + jnp.array(REL, jnp.int32)) % planes

    with jax.named_scope("temporal"):
        order = frame_order.astype(jnp.float32)[frames]
        distance = jnp.abs(order[:, None] - order[None, :])
        pair_global = (z * pairs + jnp.arange(pairs, dtype=jnp.int32)).astype(jnp.float32)
        slope = jnp.exp2(-(pair_global + 1.0) * 2.0 / HP)
        tmask = lax.dynamic_index_in_dim(temporal_mask, seq_index, 1, keepdims=False)
        tmask = tmask[:, frames][:, :, frames]
        bias_t = jnp.where(tmask > 0, -slope[:, None, None] * distance[None] * LOG2E, OFF)
        bias_t = jnp.repeat(bias_t, tokens, axis=2)[:, :, None, :]
        temporal_out = temporal_attention(temporal, bias_t)
        temporal_far = along_z(temporal_out[1:], 2)

    with jax.named_scope("spatial"):
        smask = lax.dynamic_index_in_dim(
            spatial_mask, jnp.minimum(x, pairs - 1), 0, keepdims=False
        )
        slot_frame = (z + jnp.array(REL, jnp.int32)[y]) % planes
        smask = lax.dynamic_index_in_dim(smask, slot_frame, 0, keepdims=False)
        smask = smask.reshape(chips, 2, chips, 2)
        smask = lax.dynamic_index_in_dim(smask, core, 1, keepdims=False)
        own_keys = lax.dynamic_index_in_dim(smask, core, 2, keepdims=False)
        other_keys = lax.dynamic_index_in_dim(smask, 1 - core, 2, keepdims=False)
        smask = jnp.concatenate([own_keys, other_keys], axis=1).T
        bias_s = jnp.where(smask > 0, 0.0, OFF).astype(jnp.float32)
        bias_s = jnp.pad(bias_s, ((0, 0), (0, HD - chips)))
        mine = lax.all_to_all(
            spatial.reshape(chips, tokens, 3 * HD), ("y", "x"), 0, 0, tiled=True
        )
        mine, temporal_out, temporal_far, bias_s, out_weight = lax.optimization_barrier(
            (mine, temporal_out, temporal_far, bias_s, out_weight)
        )
        other = swap_cores(mine)
        partial = spatial_attention(mine, mine, bias_s)
        spatial_out = spatial_attention(mine, other, bias_s, partial)
        spatial_out = lax.all_to_all(spatial_out, ("y", "x"), 0, 0, tiled=True)
        spatial_out = spatial_out.reshape(4, 4, tokens, HD)
        spatial_far = along_z(spatial_out[1:, :pairs], 2)

    with jax.named_scope("project"):
        own_heads, far_heads = [spatial_out, temporal_out], [spatial_far, temporal_far]
        sent = project(
            "project_sent_own_group", (1, -1), (0,), own_heads, out_weight, jnp.float32, WIDE
        )
        low, high = project(
            "project_sent", (1, -1), (1,), far_heads, out_weight, jnp.bfloat16, 24 * 1024 * 1024, sent
        )
        low = along_z(low, 1)
        high = along_z(high, -1)
        kept = project(
            "project_kept", (0,), (0, 1), own_heads + far_heads, out_weight, jnp.bfloat16, NARROW
        )
        return combine(kept, low, high, gate_mod)[None]


def solution(mesh):
    split = Mesh(mesh.devices.reshape(4, 4, 2, 4), ("y", "x", "core", "frm"))
    seq = ("y", "x", "core")
    placed = (
        P("frm", seq, None),
        P(),
        P(),
        P(),
        P(None, "frm", None, None),
        P("frm", None, None),
        P("frm", None, None, seq),
        P("frm", None, None, None),
        P("frm", None, None, None),
        P(),
    )
    return jax.shard_map(
        local, mesh=split, in_specs=placed, out_specs=P("frm", seq, None), check_vma=False
    )
```
